512 devices in a mesh: tensor: 16 (over x, z_hi), feature: 8 (over y, core), dp: 4 (over z_lo).
Axes of the slice: x: 4, y: 4, z: 16 (z_hi: 4, z_lo: 4; z = z_hi * 4 + z_lo), core: 2. Of those that a mesh axis runs over, the one named last changes fastest.
Arguments:
- mlp_input: bfloat16 [64, 4096], P(None, ('feature', 'dp')), may hold values from -6 to 6
- gate_weight: bfloat16 [4096, 28672], P(('feature', 'dp'), 'tensor'), may hold values from -0.09375 to 0.09375
- up_weight: bfloat16 [4096, 28672], P(('feature', 'dp'), 'tensor'), may hold values from -0.09375 to 0.09375
- down_weight: bfloat16 [28672, 4096], P('tensor', ('feature', 'dp')), may hold values from -0.03125 to 0.03125
- down_encoder: bfloat16 [65536, 4096], P('tensor', ('feature', 'dp')), may hold values from -6 to 6
- feature_ids: int32 [32], replicated, may hold values from 0 to 65535
- up_decoder: bfloat16 [131072, 4096], P('tensor', ('feature', 'dp')), may hold values from -0.09375 to 0.09375
- latent_ids: int32 [64, 64], replicated, may hold values from 0 to 131071, as said below
- latent_acts: float32 [64, 64], P('dp', 'tensor'), may hold values from 0.5 to 4
Outputs:
- attribution: float32 [32, 64, 64], P('feature', 'dp', 'tensor')
The draws below stay inside these ranges and needn't reach their ends.
Inputs may be any that keep to these rules, and one draw needn't show every extreme that they name: `latent_ids`: the 64 latents of one token are distinct.
All inputs are finite; a program needn't handle non-finite values.
Results may differ from the reference program's by a relative error of at most 0.0029.
Values may be sent and summed in bfloat16 or wider, within the bound.
No kernel may reach another device: no remote copies, remote signals or barrier semaphores. Data moves between devices by JAX's collectives and lax.ppermute only.
A program may use at most 64 MiB of HBM per device.

```python
import math
import jax
import jax.numpy as jnp
from jax import lax

D = 4096
FF = 28672
LAT_UP = 131072
LAT_DN = 65536
K = 64
TOK = 64
F = 32


def draw_latent_ids(key, part):
    keys = jax.random.split(key, TOK)

    def pick_latents(row_key):
        return jax.random.permutation(row_key, LAT_UP)[:K]
    return jax.vmap(pick_latents)(keys).astype(jnp.int32)


def set_ends(entries, key, low, largest):
    longest = entries.shape.index(max(entries.shape))
    spots = []
    for shift in (0, 1):
        where = [jax.random.randint(jax.random.fold_in(key, axis), (), 0, length) for axis, length in enumerate(entries.shape)]
        where[longest] = (where[longest] + shift) % entries.shape[longest]
        spots.append(tuple(where))
    return entries.at[spots[0]].set(low).at[spots[1]].set(largest)


def steps_of(rng, dims, pieces, low, top_value):
    factor_of, own = 1.0, jax.random.fold_in(rng, 6)
    for dim, blocks in pieces:
        steps = jnp.exp(jax.random.uniform(jax.random.fold_in(own, dim), (blocks,), jnp.float32, low / len(pieces), top_value / len(pieces)))
        factor_of = factor_of * jnp.repeat(steps, dims[dim] // blocks).reshape([-1 if axis == dim else 1 for axis in range(len(dims))])
    return factor_of


def noise(rng, shape, scale, limit, cuts=(), held_as=jnp.bfloat16):
    entries = scale * jax.random.normal(rng, shape, jnp.float32)
    if cuts:
        entries = entries * steps_of(rng, shape, cuts, -0.22, 0.18)
    return jnp.clip(entries, -limit, limit).astype(held_as)


def setup_inputs(seed: int = 0) -> dict:
    streams_of = jax.random.split(jax.random.key(seed), 10)
    return {
        "mlp_input": noise(streams_of[0], (TOK, D), 1.0, 6.0, ((1, 32),)),
        "gate_weight": noise(streams_of[1], (D, FF), D ** -0.5, 0.09375, ((0, 32), (1, 16))),
        "up_weight": noise(streams_of[2], (D, FF), D ** -0.5, 0.09375, ((0, 32), (1, 16))),
        "down_weight": noise(streams_of[3], (FF, D), FF ** -0.5, 0.03125, ((0, 16), (1, 32))),
        "down_encoder": noise(streams_of[4], (LAT_DN, D), 1.0, 6.0, ((0, 16), (1, 32))),
        "feature_ids": set_ends(jax.random.randint(streams_of[5], (F,), 0, LAT_DN), jax.random.fold_in(streams_of[5], 1), 0, LAT_DN - 1).astype(jnp.int32),
        "up_decoder": noise(streams_of[6], (LAT_UP, D), D ** -0.5, 0.09375, ((0, 16), (1, 32))),
        "latent_ids": draw_latent_ids(jax.random.fold_in(streams_of[9], 71), 0),
        "latent_acts": jnp.clip(jnp.exp(math.log(4.0) - 2.0794415 * jax.random.uniform(streams_of[8], (TOK, K), jnp.float32) ** steps_of(streams_of[8], (TOK, K), ((0, 4), (1, 16)), -0.2, 0.2)), 0.5, 4.0),
    }


def factors(gate_pre, up_pre):
    sigmoid_gate = jax.nn.sigmoid(gate_pre)
    gate_factor = up_pre * sigmoid_gate * (1.0 + gate_pre * (1.0 - sigmoid_gate))
    up_factor = gate_pre * sigmoid_gate
    return gate_factor, up_factor


def reference(mlp_input, gate_weight, up_weight, down_weight, down_encoder, feature_ids, up_decoder, latent_ids, latent_acts):
    gate_pre = jnp.dot(mlp_input, gate_weight, preferred_element_type=jnp.float32)
    up_pre = jnp.dot(mlp_input, up_weight, preferred_element_type=jnp.float32)
    gate_factor, up_factor = factors(gate_pre, up_pre)
    contract = (((1,), (1,)), ((), ()))
    cotangent = jnp.take(down_encoder, feature_ids, axis=0)
    neuron_grad = lax.dot_general(cotangent, down_weight, contract, preferred_element_type=jnp.float32)
    decoder_rows = jnp.take(up_decoder, latent_ids, axis=0).astype(jnp.float32)

    def per_feature(grad_row):
        grad_gate = (grad_row[None, :] * gate_factor).astype(jnp.bfloat16)
        grad_up = (grad_row[None, :] * up_factor).astype(jnp.bfloat16)
        width_grad = lax.dot_general(grad_gate, gate_weight, contract, preferred_element_type=jnp.float32)
        width_grad = width_grad + lax.dot_general(grad_up, up_weight, contract, preferred_element_type=jnp.float32)
        return jnp.einsum("td,tkd->tk", width_grad, decoder_rows, precision=lax.Precision.HIGHEST)

    attribution_raw = lax.map(per_feature, neuron_grad)
    return attribution_raw * latent_acts[None, :, :]
```

```python
import functools

import jax
import jax.numpy as jnp
from jax import lax
from jax.experimental import pallas as pl
from jax.experimental.pallas import tpu as pltpu
from jax.sharding import Mesh
from jax.sharding import PartitionSpec as P

F32 = jnp.float32
BF16 = jnp.bfloat16
CAP = 352
VMEM_LIMIT = 48 * 1024 * 1024


def nt(a, b):
    return lax.dot_general(a, b, (((1,), (1,)), ((), ())), preferred_element_type=F32)


def nn(a, b):
    return lax.dot_general(a, b, (((1,), (0,)), ((), ())), preferred_element_type=F32)


def plan_kernel(owners, dec_rows, where_ref, ids_ref, pos_ref, list_ref):
    rows, lanes = ids_ref.shape
    ids = ids_ref[...]
    owner = lax.div(ids, dec_rows)
    upto = lax.broadcasted_iota(jnp.int32, (lanes, lanes), 0) <= lax.broadcasted_iota(
        jnp.int32, (lanes, lanes), 1
    )
    upto = upto.astype(F32).astype(BF16)
    before = lax.broadcasted_iota(jnp.int32, (rows, rows), 1) < lax.broadcasted_iota(
        jnp.int32, (rows, rows), 0
    )
    before = before.astype(F32).astype(BF16)
    ones = jnp.ones((lanes, lanes), BF16)
    pos = jnp.zeros((rows, lanes), F32)
    for o in range(owners):
        hit = (owner == o).astype(F32)
        hit16 = hit.astype(BF16)
        total = nn(hit16, ones).astype(BF16)
        count = nn(hit16, upto) + nn(before, total)
        pos = pos + hit * (count - 1.0)
    pos_ref[...] = pos.astype(jnp.int32)
    rank = where_ref[0]
    start = where_ref[1] * CAP
    mine = jnp.where(owner == rank, pos - start.astype(F32), -1.0)
    local = (ids - rank * dec_rows).astype(F32)
    slot = lax.broadcasted_iota(jnp.int32, (CAP, lanes), 0).astype(F32)
    acc = jnp.zeros((CAP, lanes), F32)
    for r in range(rows):
        acc = acc + jnp.where(mine[r : r + 1, :] == slot, local[r : r + 1, :], 0.0)
    list_ref[...] = jnp.sum(acc, axis=1, keepdims=True).astype(jnp.int32)


def plan(ids, rank, turn, owners, dec_rows):
    flat = ids.reshape(-1, 128)
    pos, rows = pl.pallas_call(
        functools.partial(plan_kernel, owners, dec_rows),
        out_shape=(
            jax.ShapeDtypeStruct(flat.shape, jnp.int32),
            jax.ShapeDtypeStruct((CAP, 1), jnp.int32),
        ),
        in_specs=[
            pl.BlockSpec(memory_space=pltpu.SMEM),
            pl.BlockSpec(memory_space=pltpu.VMEM),
        ],
        out_specs=(pl.BlockSpec(memory_space=pltpu.VMEM), pl.BlockSpec(memory_space=pltpu.VMEM)),
        compiler_params=pltpu.CompilerParams(vmem_limit_bytes=VMEM_LIMIT),
    )(jnp.stack([rank, turn]).astype(jnp.int32), flat)
    return pos.reshape(-1), rows.reshape(-1)


def forward_kernel(half, core_ref, x_ref, cot_ref, gate_ref, up_ref, down_ref, rec_ref, out_ref):
    core = core_ref[0]
    tokens = x_ref.shape[0]
    features = cot_ref.shape[0]
    dblk = x_ref.shape[1]
    group = 2 * tokens + features
    x_own = x_ref[...]
    x_far = rec_ref[3 * half : 3 * half + tokens, :]
    cot_own = cot_ref[:, :dblk]
    cot_far = cot_ref[:, dblk:]
    for i in range(half // 128):
        col = pl.ds(pl.multiple_of(core * half + i * 128, 128), 128)
        far = slice(i * 128, (i + 1) * 128)
        base = i * group
        out_ref[base : base + tokens, :] = nn(x_own, gate_ref[:, col]) + nn(x_far, rec_ref[far, :])
        far = slice(half + i * 128, half + (i + 1) * 128)
        out_ref[base + tokens : base + 2 * tokens, :] = nn(x_own, up_ref[:, col]) + nn(
            x_far, rec_ref[far, :]
        )
        far = slice(2 * half + i * 128, 2 * half + (i + 1) * 128)
        out_ref[base + 2 * tokens : base + group, :] = nt(cot_own, down_ref[col, :]) + nt(
            cot_far, rec_ref[far, :]
        )
    used = (half // 128) * group
    if out_ref.shape[0] > used:
        out_ref[used:, :] = jnp.zeros((out_ref.shape[0] - used, 128), F32)


def main_kernel(
    half, tokens, features, core_ref, pre_ref, gate_ref, up_ref, rec_ref, own_ref, far_ref,
    mine_ref, theirs_ref, weight, grads,
):
    core = core_ref[0]
    step = pl.program_id(0)
    tile = own_ref.shape[0] // 64
    dblk = gate_ref.shape[0]
    group = 2 * tokens + features

    @pl.when(step == 0)
    def _():
        cols = pl.ds(pl.multiple_of(core * half, 128), half)
        weight[:dblk, :half] = gate_ref[:, cols]
        weight[:dblk, half:] = up_ref[:, cols]
        for i in range(half // 128):
            far = slice(i * 128, (i + 1) * 128)
            weight[dblk:, far] = rec_ref[far, :]
            far = slice(half + i * 128, half + (i + 1) * 128)
            weight[dblk:, far] = rec_ref[far, :]

    for i in range(half // 128):
        base = i * group
        gate_pre = pre_ref[pl.ds(pl.multiple_of(base + step * tile, 8), tile), :]
        up_pre = pre_ref[pl.ds(pl.multiple_of(base + tokens + step * tile, 8), tile), :]
        neuron = pre_ref[base + 2 * tokens : base + group, :]
        s = jax.nn.sigmoid(gate_pre)
        gate_factor = up_pre * s * (1.0 + gate_pre * (1.0 - s))
        up_factor = gate_pre * s
        for j in range(features):
            row = neuron[j : j + 1, :]
            to = slice(j * tile, (j + 1) * tile)
            grads[to, i * 128 : (i + 1) * 128] = (row * gate_factor).astype(BF16)
            grads[to, half + i * 128 : half + (i + 1) * 128] = (row * up_factor).astype(BF16)
    width = nt(grads[...], weight[...])
    high = width.astype(BF16)
    low = (width - high.astype(F32)).astype(BF16)
    dec = jnp.concatenate([own_ref[...], far_ref[...]], axis=1)
    lane = lax.broadcasted_iota(jnp.int32, (64, 128), 1)
    first = lax.broadcasted_iota(jnp.int32, (32, 128), 1) < 64
    which = lax.rem(lane, tile)
    for y in range(features // 8):
        part = slice(y * 128, (y + 1) * 128)
        both = jnp.concatenate([high[part, :], low[part, :]], axis=0)
        full = nt(dec, both)
        full = full[:, :128] + full[:, 128:]
        sel = full[:64, :]
        for t in range(1, tile):
            sel = jnp.where(which == t, full[t * 64 : (t + 1) * 64, :], sel)
        a, b = sel[:32, :], sel[32:, :]
        zero = jnp.where(first, a, pltpu.roll(b, 64, 1))
        one = jnp.where(first, pltpu.roll(a, 64, 1), b)
        keep = jnp.where(core == 0, zero, one)
        send = jnp.where(core == 0, one, zero)
        for x in range(4):
            to = pl.ds(pl.multiple_of(((x * 4 + y) * 4 + step) * 8, 8), 8)
            mine_ref[to, :] = keep[x * 8 : (x + 1) * 8, :]
            theirs_ref[to, :] = send[x * 8 : (x + 1) * 8, :]


def swap(value):
    return lax.ppermute(value, "c", [(0, 1), (1, 0)])


def on_device(
    mlp_input,
    gate_weight,
    up_weight,
    down_weight,
    down_encoder,
    feature_ids,
    up_decoder,
    latent_ids,
    latent_acts,
):
    tokens, dblk = mlp_input.shape
    half = gate_weight.shape[1] // 2
    features = feature_ids.shape[0]
    slots = latent_ids.shape[1]
    owners = 16
    core = lax.axis_index("c").astype(jnp.int32)
    rank = (lax.axis_index("x") * 4 + lax.axis_index("h")).astype(jnp.int32)
    core_arg = core[None]
    other = 1 - core

    enc_rows = down_encoder.shape[0]
    local = feature_ids - rank * enc_rows
    picker = (local[:, None] == jnp.arange(enc_rows, dtype=jnp.int32)[None, :]).astype(BF16)
    chosen = jnp.dot(picker, down_encoder, preferred_element_type=F32).astype(BF16)
    chosen_far = swap(chosen)

    def columns(w):
        part = lax.dynamic_slice(w, (0, other * half), (dblk, half))
        return part.reshape(dblk, half // 128, 128).transpose(1, 0, 2).reshape(half, 128)

    pack = jnp.concatenate(
        [
            columns(gate_weight),
            columns(up_weight),
            lax.dynamic_slice(down_weight, (other * half, 0), (half, dblk)),
            mlp_input,
        ],
        axis=0,
    )
    rec = swap(pack)

    dec_rows = up_decoder.shape[0]
    ordered = latent_ids.reshape(tokens, slots // 4, 2, 2).transpose(0, 3, 1, 2).reshape(-1)
    pos, rows = plan(ordered, rank, jnp.int32(0), owners, dec_rows)
    owner = ordered // dec_rows
    picked = jnp.take(up_decoder, rows, axis=0, mode="clip")
    packet = jnp.concatenate([picked, chosen, chosen_far], axis=0)

    def spread(value):
        return lax.all_gather(lax.all_gather(value, "h"), "x").reshape(owners, value.shape[0], 128)

    gathered = spread(packet)
    cot = jnp.sum(gathered[:, CAP:, :].astype(F32), axis=0).astype(BF16)
    cot = jnp.concatenate([cot[:features], cot[features:]], axis=1)

    used = (half // 128) * (2 * tokens + features)
    padded = -(-used // 128) * 128
    vmem = pl.BlockSpec(memory_space=pltpu.VMEM)
    smem = pl.BlockSpec(memory_space=pltpu.SMEM)
    params = pltpu.CompilerParams(vmem_limit_bytes=VMEM_LIMIT)
    part = pl.pallas_call(
        functools.partial(forward_kernel, half),
        out_shape=jax.ShapeDtypeStruct((padded, 128), F32),
        in_specs=[smem] + [vmem] * 6,
        out_specs=vmem,
        compiler_params=params,
    )(core_arg, mlp_input, cot, gate_weight, up_weight, down_weight, rec)
    part = lax.all_to_all(part.reshape(16, padded // 16, 128), ("y", "l"), 0, 0, tiled=True)
    part = jnp.sum(part, axis=0)
    pre = lax.all_to_all(
        jnp.broadcast_to(part[None], (16,) + part.shape), ("y", "l"), 0, 0, tiled=True
    ).reshape(padded, 128)

    table = gathered.reshape(owners * packet.shape[0], 128)
    place = owner * packet.shape[0] + jnp.minimum(pos, CAP - 1)
    dec = jnp.take(table, place, axis=0, mode="clip")
    rounds = jnp.max(pos) // CAP + 1

    def more(carry):
        return carry[0] < rounds

    def another(carry):
        turn, have = carry
        _, rows_now = plan(ordered, rank, turn, owners, dec_rows)
        got = spread(jnp.take(up_decoder, rows_now, axis=0, mode="clip"))
        at = pos - turn * CAP
        here = jnp.logical_and(at >= 0, at < CAP)
        at = owner * CAP + jnp.clip(at, 0, CAP - 1)
        now = jnp.take(got.reshape(owners * CAP, 128), at, axis=0, mode="clip")
        return turn + 1, jnp.where(here[:, None], now, have)

    _, dec = lax.while_loop(more, another, (jnp.int32(1), dec))
    dec_far = swap(dec)

    steps = 4
    block = dec.shape[0] // steps
    whole = lambda *shape: pl.BlockSpec(shape, lambda i: (0, 0))
    out_rows = 512
    mine, theirs = pl.pallas_call(
        functools.partial(main_kernel, half, tokens, features),
        grid=(steps,),
        out_shape=(jax.ShapeDtypeStruct((out_rows, 128), F32),) * 2,
        in_specs=[
            smem,
            whole(*pre.shape),
            whole(*gate_weight.shape),
            whole(*up_weight.shape),
            whole(*rec.shape),
            pl.BlockSpec((block, 128), lambda i: (i, 0)),
            pl.BlockSpec((block, 128), lambda i: (i, 0)),
        ],
        out_specs=(whole(out_rows, 128),) * 2,
        scratch_shapes=[
            pltpu.VMEM((2 * dblk, 2 * half), BF16),
            pltpu.VMEM((features * tokens // steps, 2 * half), BF16),
        ],
        compiler_params=params,
    )(core_arg, pre, gate_weight, up_weight, rec, dec, dec_far)

    total = mine + swap(theirs)
    total = jnp.sum(lax.all_to_all(total.reshape(16, 32, 128), ("x", "y"), 0, 0, tiled=True), axis=0)
    total = jnp.sum(lax.all_to_all(total.reshape(16, 2, 128), ("l", "h"), 0, 0, tiled=True), axis=0)
    total = total.reshape(2, 2, features // 8, tokens // 4).transpose(2, 3, 0, 1)
    return total.reshape(features // 8, tokens // 4, slots // 16) * latent_acts[None, :, :]


def solution(mesh):
    fine = Mesh(mesh.devices.reshape(4, 4, 4, 2, 4), ("x", "h", "y", "c", "l"))
    width = ("y", "c", "l")
    tensor = ("x", "h")
    in_specs = (
        P(None, width),
        P(width, tensor),
        P(width, tensor),
        P(tensor, width),
        P(tensor, width),
        P(),
        P(tensor, width),
        P(),
        P("l", tensor),
    )
    out_specs = P(("y", "c"), "l", tensor)
    return jax.shard_map(
        on_device, mesh=fine, in_specs=in_specs, out_specs=out_specs, check_vma=False
    )
```

```python
import functools

import jax
import jax.numpy as jnp
from jax import lax
from jax.experimental import pallas as pl
from jax.experimental.pallas import tpu as pltpu
from jax.sharding import Mesh
from jax.sharding import PartitionSpec as P

F32 = jnp.float32
BF16 = jnp.bfloat16
CAP = 352
VMEM_LIMIT = 48 * 1024 * 1024


def nt(a, b):
    return lax.dot_general(a, b, (((1,), (1,)), ((), ())), preferred_element_type=F32)


def nn(a, b):
    return lax.dot_general(a, b, (((1,), (0,)), ((), ())), preferred_element_type=F32)


def plan_kernel(owners, dec_rows, where_ref, ids_ref, slot_ref, list_ref, rounds_ref):
    tokens, slots = ids_ref.shape
    ids = ids_ref[...]
    ids = jnp.concatenate([ids[: tokens // 2], ids[tokens // 2 :]], axis=1)
    rows, lanes = ids.shape
    owner = lax.div(ids, dec_rows)
    upto = lax.broadcasted_iota(jnp.int32, (lanes, lanes), 0) <= lax.broadcasted_iota(
        jnp.int32, (lanes, lanes), 1
    )
    upto = upto.astype(F32).astype(BF16)
    before = lax.broadcasted_iota(jnp.int32, (rows, rows), 1) < lax.broadcasted_iota(
        jnp.int32, (rows, rows), 0
    )
    before = before.astype(F32).astype(BF16)
    ones = jnp.ones((lanes, lanes), BF16)
    pos = jnp.zeros((rows, lanes), F32)
    for o in range(owners):
        hit = (owner == o).astype(F32)
        hit16 = hit.astype(BF16)
        total = nn(hit16, ones).astype(BF16)
        count = nn(hit16, upto) + nn(before, total)
        pos = pos + hit * (count - 1.0)
    rank = where_ref[0]
    start = where_ref[1] * CAP
    at = pos.astype(jnp.int32) - start
    here = jnp.logical_and(at >= 0, at < CAP)
    late = (at >= CAP // 2).astype(jnp.int32)
    slot = late * (owners * CAP // 2) + owner * (CAP // 2) + at - late * (CAP // 2)
    slot = jnp.where(here, slot, -1)
    slot_ref[...] = jnp.concatenate([slot[:, :slots], slot[:, slots:]], axis=0)
    rounds_ref[0] = lax.div(jnp.max(pos).astype(jnp.int32), CAP) + 1
    mine = jnp.where(owner == rank, pos - start.astype(F32), -1.0)
    local = (ids - rank * dec_rows).astype(F32)
    want = lax.broadcasted_iota(jnp.int32, (CAP, lanes), 0).astype(F32)
    acc = jnp.zeros((CAP, lanes), F32)
    for r in range(rows):
        acc = acc + jnp.where(mine[r : r + 1, :] == want, local[r : r + 1, :], 0.0)
    list_ref[...] = jnp.sum(acc, axis=1, keepdims=True).astype(jnp.int32)


def plan(ids, rank, turn, owners, dec_rows):
    slot, rows, rounds = pl.pallas_call(
        functools.partial(plan_kernel, owners, dec_rows),
        out_shape=(
            jax.ShapeDtypeStruct(ids.shape, jnp.int32),
            jax.ShapeDtypeStruct((CAP, 1), jnp.int32),
            jax.ShapeDtypeStruct((1,), jnp.int32),
        ),
        in_specs=[
            pl.BlockSpec(memory_space=pltpu.SMEM),
            pl.BlockSpec(memory_space=pltpu.VMEM),
        ],
        out_specs=(
            pl.BlockSpec(memory_space=pltpu.VMEM),
            pl.BlockSpec(memory_space=pltpu.VMEM),
            pl.BlockSpec(memory_space=pltpu.SMEM),
        ),
        compiler_params=pltpu.CompilerParams(vmem_limit_bytes=VMEM_LIMIT),
    )(jnp.stack([rank, turn]).astype(jnp.int32), ids)
    return slot, rows.reshape(-1), rounds[0]


def expand_kernel(slot_ref, early_ref, late_ref, out_ref, table, block):
    size = early_ref.shape[0]
    piece = 128

    def widen(i, carry):
        at = pl.ds(pl.multiple_of(i * piece, piece), piece)
        table[at, :] = early_ref[at, :].astype(F32)
        table[pl.ds(pl.multiple_of(size + i * piece, piece), piece), :] = late_ref[at, :].astype(F32)
        return carry

    lax.fori_loop(0, size // piece, widen, 0)
    tokens, slots = slot_ref.shape

    def token(t, carry):
        for low in range(2):
            for r in range(slots // 4):
                for high in range(2):
                    src = jnp.maximum(slot_ref[t, r * 4 + high * 2 + low], 0)
                    to = low * (slots // 2) + r * 2 + high
                    block[to : to + 1, :] = table[pl.ds(src, 1), :]
        out_ref[pl.ds(pl.multiple_of(t * slots, slots), slots), :] = block[...].astype(BF16)
        return carry

    lax.fori_loop(0, tokens, token, 0)


def expand(slot, early, late):
    size = early.shape[0]
    return pl.pallas_call(
        expand_kernel,
        out_shape=jax.ShapeDtypeStruct((slot.shape[0] * slot.shape[1], 128), BF16),
        in_specs=[
            pl.BlockSpec(memory_space=pltpu.SMEM),
            pl.BlockSpec(memory_space=pltpu.VMEM),
            pl.BlockSpec(memory_space=pltpu.VMEM),
        ],
        out_specs=pl.BlockSpec(memory_space=pltpu.VMEM),
        scratch_shapes=[
            pltpu.VMEM((2 * size, 128), F32),
            pltpu.VMEM((slot.shape[1], 128), F32),
        ],
        compiler_params=pltpu.CompilerParams(vmem_limit_bytes=VMEM_LIMIT),
    )(slot, early, late)


def forward_kernel(half, core_ref, x_ref, cot_ref, gate_ref, up_ref, down_ref, rec_ref, out_ref):
    core = core_ref[0]
    tokens = x_ref.shape[0]
    features = cot_ref.shape[0]
    dblk = x_ref.shape[1]
    group = 2 * tokens + features
    x_own = x_ref[...]
    x_far = rec_ref[3 * half : 3 * half + tokens, :]
    cot_own = cot_ref[:, :dblk]
    cot_far = cot_ref[:, dblk:]
    for i in range(half // 128):
        col = pl.ds(pl.multiple_of(core * half + i * 128, 128), 128)
        far = slice(i * 128, (i + 1) * 128)
        base = i * group
        out_ref[base : base + tokens, :] = nn(x_own, gate_ref[:, col]) + nn(x_far, rec_ref[far, :])
        far = slice(half + i * 128, half + (i + 1) * 128)
        out_ref[base + tokens : base + 2 * tokens, :] = nn(x_own, up_ref[:, col]) + nn(
            x_far, rec_ref[far, :]
        )
        far = slice(2 * half + i * 128, 2 * half + (i + 1) * 128)
        out_ref[base + 2 * tokens : base + group, :] = nt(cot_own, down_ref[col, :]) + nt(
            cot_far, rec_ref[far, :]
        )
    used = (half // 128) * group
    if out_ref.shape[0] > used:
        out_ref[used:, :] = jnp.zeros((out_ref.shape[0] - used, 128), F32)


def main_kernel(
    half, tokens, features, core_ref, pre_ref, gate_ref, up_ref, rec_ref, own_ref, far_ref,
    mine_ref, theirs_ref, weight, grads,
):
    core = core_ref[0]
    step = pl.program_id(0)
    tile = own_ref.shape[0] // 64
    dblk = gate_ref.shape[0]
    group = 2 * tokens + features

    @pl.when(step == 0)
    def _():
        cols = pl.ds(pl.multiple_of(core * half, 128), half)
        weight[:dblk, :half] = gate_ref[:, cols]
        weight[:dblk, half:] = up_ref[:, cols]
        for i in range(half // 128):
            far = slice(i * 128, (i + 1) * 128)
            weight[dblk:, far] = rec_ref[far, :]
            far = slice(half + i * 128, half + (i + 1) * 128)
            weight[dblk:, far] = rec_ref[far, :]

    for i in range(half // 128):
        base = i * group
        gate_pre = pre_ref[pl.ds(pl.multiple_of(base + step * tile, 8), tile), :]
        up_pre = pre_ref[pl.ds(pl.multiple_of(base + tokens + step * tile, 8), tile), :]
        neuron = pre_ref[base + 2 * tokens : base + group, :]
        s = jax.nn.sigmoid(gate_pre)
        gate_factor = up_pre * s * (1.0 + gate_pre * (1.0 - s))
        up_factor = gate_pre * s
        for j in range(features):
            row = neuron[j : j + 1, :]
            to = slice(j * tile, (j + 1) * tile)
            grads[to, i * 128 : (i + 1) * 128] = (row * gate_factor).astype(BF16)
            grads[to, half + i * 128 : half + (i + 1) * 128] = (row * up_factor).astype(BF16)
    width = nt(grads[...], weight[...])
    high = width.astype(BF16)
    low = (width - high.astype(F32)).astype(BF16)
    dec = jnp.concatenate([own_ref[...], far_ref[...]], axis=1)
    lane = lax.broadcasted_iota(jnp.int32, (64, 128), 1)
    first = lax.broadcasted_iota(jnp.int32, (32, 128), 1) < 64
    which = lax.rem(lane, tile)
    for y in range(features // 8):
        part = slice(y * 128, (y + 1) * 128)
        both = jnp.concatenate([high[part, :], low[part, :]], axis=0)
        full = nt(dec, both)
        full = full[:, :128] + full[:, 128:]
        sel = full[:64, :]
        for t in range(1, tile):
            sel = jnp.where(which == t, full[t * 64 : (t + 1) * 64, :], sel)
        a, b = sel[:32, :], sel[32:, :]
        zero = jnp.where(first, a, pltpu.roll(b, 64, 1))
        one = jnp.where(first, pltpu.roll(a, 64, 1), b)
        keep = jnp.where(core == 0, zero, one)
        send = jnp.where(core == 0, one, zero)
        for x in range(4):
            to = pl.ds(pl.multiple_of(((x * 4 + y) * 4 + step) * 8, 8), 8)
            mine_ref[to, :] = keep[x * 8 : (x + 1) * 8, :]
            theirs_ref[to, :] = send[x * 8 : (x + 1) * 8, :]


def swap(value):
    return lax.ppermute(value, "c", [(0, 1), (1, 0)])


def on_device(
    mlp_input,
    gate_weight,
    up_weight,
    down_weight,
    down_encoder,
    feature_ids,
    up_decoder,
    latent_ids,
    latent_acts,
):
    tokens, dblk = mlp_input.shape
    half = gate_weight.shape[1] // 2
    features = feature_ids.shape[0]
    slots = latent_ids.shape[1]
    owners = 16
    core = lax.axis_index("c").astype(jnp.int32)
    rank = (lax.axis_index("x") * 4 + lax.axis_index("h")).astype(jnp.int32)
    core_arg = core[None]
    other = 1 - core

    enc_rows = down_encoder.shape[0]
    local = feature_ids - rank * enc_rows
    picker = (local[:, None] == jnp.arange(enc_rows, dtype=jnp.int32)[None, :]).astype(BF16)
    chosen = jnp.dot(picker, down_encoder, preferred_element_type=F32).astype(BF16)
    chosen_far = swap(chosen)

    def columns(w):
        part = lax.dynamic_slice(w, (0, other * half), (dblk, half))
        return part.reshape(dblk, half // 128, 128).transpose(1, 0, 2).reshape(half, 128)

    pack = jnp.concatenate(
        [
            columns(gate_weight),
            columns(up_weight),
            lax.dynamic_slice(down_weight, (other * half, 0), (half, dblk)),
            mlp_input,
        ],
        axis=0,
    )
    rec = swap(pack)

    dec_rows = up_decoder.shape[0]
    slot, rows, rounds = plan(latent_ids, rank, jnp.int32(0), owners, dec_rows)
    picked = jnp.take(up_decoder, rows, axis=0, mode="clip")
    packet = lax.all_gather(jnp.concatenate([picked, chosen, chosen_far], axis=0), "h")

    def spread(value):
        return lax.all_gather(value, "x").reshape(owners * value.shape[1], 128)

    cot = lax.all_gather(packet[:, CAP:, :], "x").reshape(owners, 2 * features, 128)
    cot = jnp.sum(cot.astype(F32), axis=0).astype(BF16)
    cot = jnp.concatenate([cot[:features], cot[features:]], axis=1)

    used = (half // 128) * (2 * tokens + features)
    padded = -(-used // 128) * 128
    vmem = pl.BlockSpec(memory_space=pltpu.VMEM)
    smem = pl.BlockSpec(memory_space=pltpu.SMEM)
    params = pltpu.CompilerParams(vmem_limit_bytes=VMEM_LIMIT)
    part = pl.pallas_call(
        functools.partial(forward_kernel, half),
        out_shape=jax.ShapeDtypeStruct((padded, 128), F32),
        in_specs=[smem] + [vmem] * 6,
        out_specs=vmem,
        compiler_params=params,
    )(core_arg, mlp_input, cot, gate_weight, up_weight, down_weight, rec)
    part, packet = lax.optimization_barrier((part, packet))
    part = lax.all_to_all(part.reshape(16, padded // 16, 128), ("y", "l"), 0, 0, tiled=True)
    early, late = spread(packet[:, : CAP // 2, :]), spread(packet[:, CAP // 2 : CAP, :])
    part = jnp.sum(part, axis=0)
    part, early, late = lax.optimization_barrier((part, early, late))
    pre = lax.all_to_all(
        jnp.broadcast_to(part[None], (16,) + part.shape), ("y", "l"), 0, 0, tiled=True
    ).reshape(padded, 128)

    dec = expand(slot, early, late)

    def more(carry):
        return carry[0] < rounds

    def another(carry):
        turn, have = carry
        slot_now, rows_now, _ = plan(latent_ids, rank, turn, owners, dec_rows)
        got = lax.all_gather(jnp.take(up_decoder, rows_now, axis=0, mode="clip"), "h")
        now = expand(slot_now, spread(got[:, : CAP // 2, :]), spread(got[:, CAP // 2 :, :]))
        here = slot_now.reshape(tokens, slots // 4, 2, 2).transpose(0, 3, 1, 2).reshape(-1, 1)
        return turn + 1, jnp.where(here >= 0, now, have)

    _, dec = lax.while_loop(more, another, (jnp.int32(1), dec))
    dec_far = swap(dec)

    steps = 4
    block = dec.shape[0] // steps
    whole = lambda *shape: pl.BlockSpec(shape, lambda i: (0, 0))
    out_rows = 512
    mine, theirs = pl.pallas_call(
        functools.partial(main_kernel, half, tokens, features),
        grid=(steps,),
        out_shape=(jax.ShapeDtypeStruct((out_rows, 128), F32),) * 2,
        in_specs=[
            smem,
            whole(*pre.shape),
            whole(*gate_weight.shape),
            whole(*up_weight.shape),
            whole(*rec.shape),
            pl.BlockSpec((block, 128), lambda i: (i, 0)),
            pl.BlockSpec((block, 128), lambda i: (i, 0)),
        ],
        out_specs=(whole(out_rows, 128),) * 2,
        scratch_shapes=[
            pltpu.VMEM((2 * dblk, 2 * half), BF16),
            pltpu.VMEM((features * tokens // steps, 2 * half), BF16),
        ],
        compiler_params=params,
    )(core_arg, pre, gate_weight, up_weight, rec, dec, dec_far)

    total = mine + swap(theirs)
    total = jnp.sum(lax.all_to_all(total.reshape(16, 32, 128), ("x", "y"), 0, 0, tiled=True), axis=0)
    total = jnp.sum(lax.all_to_all(total.reshape(16, 2, 128), ("l", "h"), 0, 0, tiled=True), axis=0)
    total = total.reshape(2, 2, features // 8, tokens // 4).transpose(2, 3, 0, 1)
    return total.reshape(features // 8, tokens // 4, slots // 16) * latent_acts[None, :, :]


def solution(mesh):
    fine = Mesh(mesh.devices.reshape(4, 4, 4, 2, 4), ("x", "h", "y", "c", "l"))
    width = ("y", "c", "l")
    tensor = ("x", "h")
    in_specs = (
        P(None, width),
        P(width, tensor),
        P(width, tensor),
        P(tensor, width),
        P(tensor, width),
        P(),
        P(tensor, width),
        P(),
        P("l", tensor),
    )
    out_specs = P(("y", "c"), "l", tensor)
    return jax.shard_map(
        on_device, mesh=fine, in_specs=in_specs, out_specs=out_specs, check_vma=False
    )
```

```python
import functools

import jax
import jax.numpy as jnp
from jax import lax
from jax.experimental import pallas as pl
from jax.experimental.pallas import tpu as pltpu
from jax.sharding import Mesh
from jax.sharding import PartitionSpec as P

F32 = jnp.float32
BF16 = jnp.bfloat16
CAP = 352
MIB = 1024 * 1024


def nt(a, b):
    return lax.dot_general(a, b, (((1,), (1,)), ((), ())), preferred_element_type=F32)


def nn(a, b):
    return lax.dot_general(a, b, (((1,), (0,)), ((), ())), preferred_element_type=F32)


def plan_kernel(owners, dec_rows, where_ref, ids_ref, slot_ref, list_ref, rounds_ref):
    tokens, slots = ids_ref.shape
    ids = ids_ref[...]
    ids = jnp.concatenate([ids[: tokens // 2], ids[tokens // 2 :]], axis=1)
    rows, lanes = ids.shape
    owner = lax.div(ids, dec_rows)
    upto = lax.broadcasted_iota(jnp.int32, (lanes, lanes), 0) <= lax.broadcasted_iota(
        jnp.int32, (lanes, lanes), 1
    )
    upto = upto.astype(F32).astype(BF16)
    before = lax.broadcasted_iota(jnp.int32, (rows, rows), 1) < lax.broadcasted_iota(
        jnp.int32, (rows, rows), 0
    )
    before = before.astype(F32).astype(BF16)
    ones = jnp.ones((lanes, lanes), BF16)
    pos = jnp.zeros((rows, lanes), F32)
    for o in range(owners):
        hit = (owner == o).astype(F32)
        hit16 = hit.astype(BF16)
        total = nn(hit16, ones).astype(BF16)
        count = nn(hit16, upto) + nn(before, total)
        pos = pos + hit * (count - 1.0)
    rank = where_ref[0]
    start = where_ref[1] * CAP
    at = pos.astype(jnp.int32) - start
    here = jnp.logical_and(at >= 0, at < CAP)
    slot = jnp.where(here, lax.bitwise_xor(owner, rank) * CAP + at, -1)
    slot_ref[...] = jnp.concatenate([slot[:, :slots], slot[:, slots:]], axis=0)
    rounds_ref[0] = lax.div(jnp.max(pos).astype(jnp.int32), CAP) + 1
    mine = jnp.where(owner == rank, pos - start.astype(F32), -1.0)
    local = (ids - rank * dec_rows).astype(F32)
    want = lax.broadcasted_iota(jnp.int32, (CAP, lanes), 0).astype(F32)
    acc = jnp.zeros((CAP, lanes), F32)
    for r in range(rows):
        acc = acc + jnp.where(mine[r : r + 1, :] == want, local[r : r + 1, :], 0.0)
    list_ref[...] = jnp.sum(acc, axis=1, keepdims=True).astype(jnp.int32)


def plan(ids, rank, turn, owners, dec_rows):
    slot, rows, rounds = pl.pallas_call(
        functools.partial(plan_kernel, owners, dec_rows),
        out_shape=(
            jax.ShapeDtypeStruct(ids.shape, jnp.int32),
            jax.ShapeDtypeStruct((CAP, 1), jnp.int32),
            jax.ShapeDtypeStruct((1,), jnp.int32),
        ),
        in_specs=[
            pl.BlockSpec(memory_space=pltpu.SMEM),
            pl.BlockSpec(memory_space=pltpu.VMEM),
        ],
        out_specs=(
            pl.BlockSpec(memory_space=pltpu.VMEM),
            pl.BlockSpec(memory_space=pltpu.VMEM),
            pl.BlockSpec(memory_space=pltpu.SMEM),
        ),
        compiler_params=pltpu.CompilerParams(vmem_limit_bytes=4 * MIB),
    )(jnp.stack([rank, turn]).astype(jnp.int32), ids)
    return slot, rows.reshape(-1), rounds[0]


def expand_kernel(slot_ref, *refs):
    parts, (out_ref, table, block) = refs[:-3], refs[-3:]
    size = parts[0].shape[0]
    piece = 128

    def widen(i, carry):
        for p, ref in enumerate(parts):
            to = pl.ds(pl.multiple_of(p * size + i * piece, piece), piece)
            table[to, :] = ref[pl.ds(pl.multiple_of(i * piece, piece), piece), :].astype(F32)
        return carry

    lax.fori_loop(0, size // piece, widen, 0)
    tokens, slots = slot_ref.shape

    def token(t, carry):
        for low in range(2):
            for r in range(slots // 4):
                for high in range(2):
                    src = jnp.maximum(slot_ref[t, r * 4 + high * 2 + low], 0)
                    to = low * (slots // 2) + r * 2 + high
                    block[to : to + 1, :] = table[pl.ds(src, 1), :]
        out_ref[pl.ds(pl.multiple_of(t * slots, slots), slots), :] = block[...].astype(BF16)
        return carry

    lax.fori_loop(0, tokens, token, 0)


def expand(slot, parts):
    size = parts[0].shape[0]
    vmem = pl.BlockSpec(memory_space=pltpu.VMEM)
    return pl.pallas_call(
        expand_kernel,
        out_shape=jax.ShapeDtypeStruct((slot.shape[0] * slot.shape[1], 128), BF16),
        in_specs=[pl.BlockSpec(memory_space=pltpu.SMEM)] + [vmem] * len(parts),
        out_specs=vmem,
        scratch_shapes=[
            pltpu.VMEM((len(parts) * size, 128), F32),
            pltpu.VMEM((slot.shape[1], 128), F32),
        ],
        compiler_params=pltpu.CompilerParams(vmem_limit_bytes=12 * MIB),
    )(slot, *parts)


def exchange(value, axis):
    return [value] + [
        lax.ppermute(value, axis, [(i, i ^ m) for i in range(4)]) for m in range(1, 4)
    ]


def column_blocks(value):
    return jnp.concatenate(exchange(value, "h"), axis=0)


def forward_kernel(half, core_ref, x_ref, cot_ref, gate_ref, up_ref, down_ref, rec_ref, out_ref):
    core = core_ref[0]
    tokens = x_ref.shape[0]
    features = cot_ref.shape[0]
    dblk = x_ref.shape[1]
    group = 2 * tokens + features
    x_own = x_ref[...]
    x_far = rec_ref[3 * half : 3 * half + tokens, :]
    cot_own = cot_ref[:, :dblk]
    cot_far = cot_ref[:, dblk:]
    for i in range(half // 128):
        col = pl.ds(pl.multiple_of(core * half + i * 128, 128), 128)
        far = slice(i * 128, (i + 1) * 128)
        base = i * group
        out_ref[base : base + tokens, :] = nn(x_own, gate_ref[:, col]) + nn(x_far, rec_ref[far, :])
        far = slice(half + i * 128, half + (i + 1) * 128)
        out_ref[base + tokens : base + 2 * tokens, :] = nn(x_own, up_ref[:, col]) + nn(
            x_far, rec_ref[far, :]
        )
        far = slice(2 * half + i * 128, 2 * half + (i + 1) * 128)
        out_ref[base + 2 * tokens : base + group, :] = nt(cot_own, down_ref[col, :]) + nt(
            cot_far, rec_ref[far, :]
        )
    used = (half // 128) * group
    if out_ref.shape[0] > used:
        out_ref[used:, :] = jnp.zeros((out_ref.shape[0] - used, 128), F32)


def main_kernel(
    half, tokens, features, core_ref, pre_ref, gate_ref, up_ref, rec_ref, own_ref, far_ref,
    mine_ref, theirs_ref, weight, grads,
):
    core = core_ref[0]
    step = pl.program_id(0)
    tile = own_ref.shape[0] // 64
    dblk = gate_ref.shape[0]
    group = 2 * tokens + features

    @pl.when(step == 0)
    def _():
        cols = pl.ds(pl.multiple_of(core * half, 128), half)
        weight[:dblk, :half] = gate_ref[:, cols]
        weight[:dblk, half:] = up_ref[:, cols]
        for i in range(half // 128):
            far = slice(i * 128, (i + 1) * 128)
            weight[dblk:, far] = rec_ref[far, :]
            far = slice(half + i * 128, half + (i + 1) * 128)
            weight[dblk:, far] = rec_ref[far, :]

    for i in range(half // 128):
        base = i * group
        gate_pre = pre_ref[pl.ds(pl.multiple_of(base + step * tile, 8), tile), :]
        up_pre = pre_ref[pl.ds(pl.multiple_of(base + tokens + step * tile, 8), tile), :]
        neuron = pre_ref[base + 2 * tokens : base + group, :]
        s = jax.nn.sigmoid(gate_pre)
        gate_factor = up_pre * s * (1.0 + gate_pre * (1.0 - s))
        up_factor = gate_pre * s
        for j in range(features):
            row = neuron[j : j + 1, :]
            to = slice(j * tile, (j + 1) * tile)
            grads[to, i * 128 : (i + 1) * 128] = (row * gate_factor).astype(BF16)
            grads[to, half + i * 128 : half + (i + 1) * 128] = (row * up_factor).astype(BF16)
    width = nt(grads[...], weight[...])
    high = width.astype(BF16)
    low = (width - high.astype(F32)).astype(BF16)
    dec = jnp.concatenate([own_ref[...], far_ref[...]], axis=1)
    lane = lax.broadcasted_iota(jnp.int32, (64, 128), 1)
    first = lax.broadcasted_iota(jnp.int32, (32, 128), 1) < 64
    which = lax.rem(lane, tile)
    for y in range(features // 8):
        part = slice(y * 128, (y + 1) * 128)
        both = jnp.concatenate([high[part, :], low[part, :]], axis=0)
        full = nt(dec, both)
        full = full[:, :128] + full[:, 128:]
        sel = full[:64, :]
        for t in range(1, tile):
            sel = jnp.where(which == t, full[t * 64 : (t + 1) * 64, :], sel)
        a, b = sel[:32, :], sel[32:, :]
        zero = jnp.where(first, a, pltpu.roll(b, 64, 1))
        one = jnp.where(first, pltpu.roll(a, 64, 1), b)
        keep = jnp.where(core == 0, zero, one)
        send = jnp.where(core == 0, one, zero)
        for x in range(4):
            to = pl.ds(pl.multiple_of(((x * 4 + y) * 4 + step) * 8, 8), 8)
            mine_ref[to, :] = keep[x * 8 : (x + 1) * 8, :]
            theirs_ref[to, :] = send[x * 8 : (x + 1) * 8, :]


def swap(value):
    return lax.ppermute(value, "c", [(0, 1), (1, 0)])


def on_device(
    mlp_input,
    gate_weight,
    up_weight,
    down_weight,
    down_encoder,
    feature_ids,
    up_decoder,
    latent_ids,
    latent_acts,
):
    tokens, dblk = mlp_input.shape
    half = gate_weight.shape[1] // 2
    features = feature_ids.shape[0]
    slots = latent_ids.shape[1]
    owners = 16
    core = lax.axis_index("c").astype(jnp.int32)
    rank = (lax.axis_index("x") * 4 + lax.axis_index("h")).astype(jnp.int32)
    core_arg = core[None]
    other = 1 - core

    enc_rows = down_encoder.shape[0]
    local = feature_ids - rank * enc_rows
    picker = (local[:, None] == jnp.arange(enc_rows, dtype=jnp.int32)[None, :]).astype(BF16)
    chosen = jnp.dot(picker, down_encoder, preferred_element_type=F32).astype(BF16)
    chosen, other = lax.optimization_barrier((chosen, other))
    chosen = jnp.concatenate([chosen, swap(chosen)], axis=0)
    cot = lax.all_to_all(
        jnp.broadcast_to(chosen[None], (owners,) + chosen.shape), ("x", "h"), 0, 0, tiled=True
    )

    def columns(w):
        part = lax.dynamic_slice(w, (0, other * half), (dblk, half))
        return part.reshape(dblk, half // 128, 128).transpose(1, 0, 2).reshape(half, 128)

    pack = jnp.concatenate(
        [
            columns(gate_weight),
            columns(up_weight),
            lax.dynamic_slice(down_weight, (other * half, 0), (half, dblk)),
            mlp_input,
        ],
        axis=0,
    )
    rec = swap(pack)

    dec_rows = up_decoder.shape[0]
    latent_ids, chosen = lax.optimization_barrier((latent_ids, chosen))
    slot, rows, rounds = plan(latent_ids, rank, jnp.int32(0), owners, dec_rows)
    picked = jnp.take(up_decoder, rows, axis=0, mode="clip")
    column = column_blocks(picked)

    cot = jnp.sum(cot.astype(F32), axis=0).astype(BF16)
    cot = jnp.concatenate([cot[:features], cot[features:]], axis=1)

    used = (half // 128) * (2 * tokens + features)
    padded = -(-used // 128) * 128
    vmem = pl.BlockSpec(memory_space=pltpu.VMEM)
    smem = pl.BlockSpec(memory_space=pltpu.SMEM)
    part = pl.pallas_call(
        functools.partial(forward_kernel, half),
        out_shape=jax.ShapeDtypeStruct((padded, 128), F32),
        in_specs=[smem] + [vmem] * 6,
        out_specs=vmem,
        compiler_params=pltpu.CompilerParams(vmem_limit_bytes=8 * MIB),
    )(core_arg, mlp_input, cot, gate_weight, up_weight, down_weight, rec)
    part, column = lax.optimization_barrier((part, column))
    part = lax.all_to_all(part.reshape(16, padded // 16, 128), ("y", "l"), 0, 0, tiled=True)
    parts = exchange(column, "x")
    part = jnp.sum(part, axis=0)
    part, slot = lax.optimization_barrier((part, slot))
    pre = lax.all_to_all(
        jnp.broadcast_to(part[None], (16,) + part.shape), ("y", "l"), 0, 0, tiled=True
    ).reshape(padded, 128)

    dec = expand(slot, parts)

    def more(carry):
        return carry[0] < rounds

    def another(carry):
        turn, have = carry
        slot_now, rows_now, _ = plan(latent_ids, rank, turn, owners, dec_rows)
        taken = jnp.take(up_decoder, rows_now, axis=0, mode="clip")
        now = expand(slot_now, exchange(column_blocks(taken), "x"))
        here = slot_now.reshape(tokens, slots // 4, 2, 2).transpose(0, 3, 1, 2).reshape(-1, 1)
        return turn + 1, jnp.where(here >= 0, now, have)

    _, dec = lax.while_loop(more, another, (jnp.int32(1), dec))
    dec_far = swap(dec)

    steps = 4
    block = dec.shape[0] // steps
    whole = lambda *shape: pl.BlockSpec(shape, lambda i: (0, 0))
    out_rows = 512
    mine, theirs = pl.pallas_call(
        functools.partial(main_kernel, half, tokens, features),
        grid=(steps,),
        out_shape=(jax.ShapeDtypeStruct((out_rows, 128), F32),) * 2,
        in_specs=[
            smem,
            whole(*pre.shape),
            whole(*gate_weight.shape),
            whole(*up_weight.shape),
            whole(*rec.shape),
            pl.BlockSpec((block, 128), lambda i: (i, 0)),
            pl.BlockSpec((block, 128), lambda i: (i, 0)),
        ],
        out_specs=(whole(out_rows, 128),) * 2,
        scratch_shapes=[
            pltpu.VMEM((2 * dblk, 2 * half), BF16),
            pltpu.VMEM((features * tokens // steps, 2 * half), BF16),
        ],
        compiler_params=pltpu.CompilerParams(vmem_limit_bytes=20 * MIB),
    )(core_arg, pre, gate_weight, up_weight, rec, dec, dec_far)

    total = mine + swap(theirs)
    total = jnp.sum(lax.all_to_all(total.reshape(16, 32, 128), ("x", "y"), 0, 0, tiled=True), axis=0)
    total = jnp.sum(lax.all_to_all(total.reshape(16, 2, 128), ("l", "h"), 0, 0, tiled=True), axis=0)
    total = total.reshape(2, 2, features // 8, tokens // 4).transpose(2, 3, 0, 1)
    return total.reshape(features // 8, tokens // 4, slots // 16) * latent_acts[None, :, :]


def solution(mesh):
    fine = Mesh(mesh.devices.reshape(4, 4, 4, 2, 4), ("x", "h", "y", "c", "l"))
    width = ("y", "c", "l")
    tensor = ("x", "h")
    in_specs = (
        P(None, width),
        P(width, tensor),
        P(width, tensor),
        P(tensor, width),
        P(tensor, width),
        P(),
        P(tensor, width),
        P(),
        P("l", tensor),
    )
    out_specs = P(("y", "c"), "l", tensor)
    return jax.shard_map(
        on_device, mesh=fine, in_specs=in_specs, out_specs=out_specs, check_vma=False
    )
```

```python
import functools

import jax
import jax.numpy as jnp
from jax import lax
from jax.experimental import pallas as pl
from jax.experimental.pallas import tpu as pltpu
from jax.sharding import Mesh
from jax.sharding import PartitionSpec as P

F32 = jnp.float32
BF16 = jnp.bfloat16
CAP = 352
MIB = 1024 * 1024


def nt(a, b):
    return lax.dot_general(a, b, (((1,), (1,)), ((), ())), preferred_element_type=F32)


def nn(a, b):
    return lax.dot_general(a, b, (((1,), (0,)), ((), ())), preferred_element_type=F32)


def plan_kernel(owners, dec_rows, where_ref, ids_ref, slot_ref, list_ref, rounds_ref):
    tokens, slots = ids_ref.shape
    ids = ids_ref[...]
    ids = jnp.concatenate([ids[: tokens // 2], ids[tokens // 2 :]], axis=1)
    rows, lanes = ids.shape
    owner = lax.div(ids, dec_rows)
    upto = lax.broadcasted_iota(jnp.int32, (lanes, lanes), 0) <= lax.broadcasted_iota(
        jnp.int32, (lanes, lanes), 1
    )
    upto = upto.astype(F32).astype(BF16)
    before = lax.broadcasted_iota(jnp.int32, (rows, rows), 1) < lax.broadcasted_iota(
        jnp.int32, (rows, rows), 0
    )
    before = before.astype(F32).astype(BF16)
    ones = jnp.ones((lanes, lanes), BF16)
    pos = jnp.zeros((rows, lanes), F32)
    for o in range(owners):
        hit = (owner == o).astype(F32)
        hit16 = hit.astype(BF16)
        total = nn(hit16, ones).astype(BF16)
        count = nn(hit16, upto) + nn(before, total)
        pos = pos + hit * (count - 1.0)
    rank = where_ref[0]
    start = where_ref[1] * CAP
    at = pos.astype(jnp.int32) - start
    here = jnp.logical_and(at >= 0, at < CAP)
    slot = jnp.where(here, lax.bitwise_xor(owner, rank) * CAP + at, -1)
    slot_ref[...] = jnp.concatenate([slot[:, :slots], slot[:, slots:]], axis=0)
    rounds_ref[0] = lax.div(jnp.max(pos).astype(jnp.int32), CAP) + 1
    mine = jnp.where(owner == rank, pos - start.astype(F32), -1.0)
    local = (ids - rank * dec_rows).astype(F32)
    want = lax.broadcasted_iota(jnp.int32, (CAP, lanes), 0).astype(F32)
    acc = jnp.zeros((CAP, lanes), F32)
    for r in range(rows):
        acc = acc + jnp.where(mine[r : r + 1, :] == want, local[r : r + 1, :], 0.0)
    list_ref[...] = jnp.sum(acc, axis=1, keepdims=True).astype(jnp.int32)


def plan(ids, rank, turn, owners, dec_rows):
    slot, rows, rounds = pl.pallas_call(
        functools.partial(plan_kernel, owners, dec_rows),
        out_shape=(
            jax.ShapeDtypeStruct(ids.shape, jnp.int32),
            jax.ShapeDtypeStruct((CAP, 1), jnp.int32),
            jax.ShapeDtypeStruct((1,), jnp.int32),
        ),
        in_specs=[
            pl.BlockSpec(memory_space=pltpu.SMEM),
            pl.BlockSpec(memory_space=pltpu.VMEM),
        ],
        out_specs=(
            pl.BlockSpec(memory_space=pltpu.VMEM),
            pl.BlockSpec(memory_space=pltpu.VMEM),
            pl.BlockSpec(memory_space=pltpu.SMEM),
        ),
        compiler_params=pltpu.CompilerParams(vmem_limit_bytes=4 * MIB),
    )(jnp.stack([rank, turn]).astype(jnp.int32), ids)
    return slot, rows.reshape(-1), rounds[0]


def expand_kernel(slot_ref, *refs):
    parts, (out_ref, table, block) = refs[:-3], refs[-3:]
    size = parts[0].shape[0]
    piece = 128

    def widen(i, carry):
        for p, ref in enumerate(parts):
            to = pl.ds(pl.multiple_of(p * size + i * piece, piece), piece)
            table[to, :] = ref[pl.ds(pl.multiple_of(i * piece, piece), piece), :].astype(F32)
        return carry

    lax.fori_loop(0, size // piece, widen, 0)
    tokens, slots = slot_ref.shape

    def token(t, carry):
        for low in range(2):
            for r in range(slots // 4):
                for high in range(2):
                    src = jnp.maximum(slot_ref[t, r * 4 + high * 2 + low], 0)
                    to = low * (slots // 2) + r * 2 + high
                    block[to : to + 1, :] = table[pl.ds(src, 1), :]
        out_ref[pl.ds(pl.multiple_of(t * slots, slots), slots), :] = block[...].astype(BF16)
        return carry

    lax.fori_loop(0, tokens, token, 0)


def expand(slot, parts):
    size = parts[0].shape[0]
    vmem = pl.BlockSpec(memory_space=pltpu.VMEM)
    return pl.pallas_call(
        expand_kernel,
        out_shape=jax.ShapeDtypeStruct((slot.shape[0] * slot.shape[1], 128), BF16),
        in_specs=[pl.BlockSpec(memory_space=pltpu.SMEM)] + [vmem] * len(parts),
        out_specs=vmem,
        scratch_shapes=[
            pltpu.VMEM((len(parts) * size, 128), F32),
            pltpu.VMEM((slot.shape[1], 128), F32),
        ],
        compiler_params=pltpu.CompilerParams(vmem_limit_bytes=12 * MIB),
    )(slot, *parts)


def exchange(value, axis):
    return [value] + [
        lax.ppermute(value, axis, [(i, i ^ m) for i in range(4)]) for m in range(1, 4)
    ]


def after(value, other):
    return lax.optimization_barrier((value, other))[0]


def forward_kernel(half, core_ref, x_ref, cot_ref, gate_ref, up_ref, down_ref, rec_ref, out_ref):
    core = core_ref[0]
    tokens = x_ref.shape[0]
    features = cot_ref.shape[0]
    dblk = x_ref.shape[1]
    group = 2 * tokens + features
    x_own = x_ref[...]
    x_far = rec_ref[3 * half : 3 * half + tokens, :]
    cot_own = cot_ref[:, :dblk]
    cot_far = cot_ref[:, dblk:]
    for i in range(half // 128):
        col = pl.ds(pl.multiple_of(core * half + i * 128, 128), 128)
        far = slice(i * 128, (i + 1) * 128)
        base = i * group
        out_ref[base : base + tokens, :] = nn(x_own, gate_ref[:, col]) + nn(x_far, rec_ref[far, :])
        far = slice(half + i * 128, half + (i + 1) * 128)
        out_ref[base + tokens : base + 2 * tokens, :] = nn(x_own, up_ref[:, col]) + nn(
            x_far, rec_ref[far, :]
        )
        far = slice(2 * half + i * 128, 2 * half + (i + 1) * 128)
        out_ref[base + 2 * tokens : base + group, :] = nt(cot_own, down_ref[col, :]) + nt(
            cot_far, rec_ref[far, :]
        )
    used = (half // 128) * group
    if out_ref.shape[0] > used:
        out_ref[used:, :] = jnp.zeros((out_ref.shape[0] - used, 128), F32)


def main_kernel(
    half, tokens, features, core_ref, pre_ref, gate_ref, up_ref, rec_ref, own_ref, far_ref,
    mine_ref, theirs_ref, weight, grads,
):
    core = core_ref[0]
    step = pl.program_id(0)
    tile = own_ref.shape[0] // 64
    dblk = gate_ref.shape[0]
    group = 2 * tokens + features

    @pl.when(step == 0)
    def _():
        cols = pl.ds(pl.multiple_of(core * half, 128), half)
        weight[:dblk, :half] = gate_ref[:, cols]
        weight[:dblk, half:] = up_ref[:, cols]
        for i in range(half // 128):
            far = slice(i * 128, (i + 1) * 128)
            weight[dblk:, far] = rec_ref[far, :]
            far = slice(half + i * 128, half + (i + 1) * 128)
            weight[dblk:, far] = rec_ref[far, :]

    for i in range(half // 128):
        base = i * group
        gate_pre = pre_ref[pl.ds(pl.multiple_of(base + step * tile, 8), tile), :]
        up_pre = pre_ref[pl.ds(pl.multiple_of(base + tokens + step * tile, 8), tile), :]
        neuron = pre_ref[base + 2 * tokens : base + group, :]
        s = jax.nn.sigmoid(gate_pre)
        gate_factor = up_pre * s * (1.0 + gate_pre * (1.0 - s))
        up_factor = gate_pre * s
        for j in range(features):
            row = neuron[j : j + 1, :]
            to = slice(j * tile, (j + 1) * tile)
            grads[to, i * 128 : (i + 1) * 128] = (row * gate_factor).astype(BF16)
            grads[to, half + i * 128 : half + (i + 1) * 128] = (row * up_factor).astype(BF16)
    width = nt(grads[...], weight[...])
    high = width.astype(BF16)
    low = (width - high.astype(F32)).astype(BF16)
    dec = jnp.concatenate([own_ref[...], far_ref[...]], axis=1)
    lane = lax.broadcasted_iota(jnp.int32, (64, 128), 1)
    first = lax.broadcasted_iota(jnp.int32, (32, 128), 1) < 64
    which = lax.rem(lane, tile)
    for y in range(features // 8):
        part = slice(y * 128, (y + 1) * 128)
        both = jnp.concatenate([high[part, :], low[part, :]], axis=0)
        full = nt(dec, both)
        full = full[:, :128] + full[:, 128:]
        sel = full[:64, :]
        for t in range(1, tile):
            sel = jnp.where(which == t, full[t * 64 : (t + 1) * 64, :], sel)
        a, b = sel[:32, :], sel[32:, :]
        zero = jnp.where(first, a, pltpu.roll(b, 64, 1))
        one = jnp.where(first, pltpu.roll(a, 64, 1), b)
        keep = jnp.where(core == 0, zero, one)
        send = jnp.where(core == 0, one, zero)
        for x in range(4):
            to = pl.ds(pl.multiple_of(((x * 4 + y) * 4 + step) * 8, 8), 8)
            mine_ref[to, :] = keep[x * 8 : (x + 1) * 8, :]
            theirs_ref[to, :] = send[x * 8 : (x + 1) * 8, :]


def swap(value):
    return lax.ppermute(value, "c", [(0, 1), (1, 0)])


def on_device(
    mlp_input,
    gate_weight,
    up_weight,
    down_weight,
    down_encoder,
    feature_ids,
    up_decoder,
    latent_ids,
    latent_acts,
):
    tokens, dblk = mlp_input.shape
    half = gate_weight.shape[1] // 2
    features = feature_ids.shape[0]
    slots = latent_ids.shape[1]
    owners = 16
    core = lax.axis_index("c").astype(jnp.int32)
    rank = (lax.axis_index("x") * 4 + lax.axis_index("h")).astype(jnp.int32)
    core_arg = core[None]
    other = 1 - core

    enc_rows = down_encoder.shape[0]
    local = feature_ids - rank * enc_rows
    picker = (local[:, None] == jnp.arange(enc_rows, dtype=jnp.int32)[None, :]).astype(BF16)
    chosen = jnp.dot(picker, down_encoder, preferred_element_type=F32).astype(BF16)
    other = after(other, chosen)
    chosen = jnp.concatenate([chosen, swap(chosen)], axis=0)
    cot = lax.all_to_all(
        jnp.broadcast_to(chosen[None], (owners,) + chosen.shape), ("x", "h"), 0, 0, tiled=True
    )

    def columns(w):
        part = lax.dynamic_slice(w, (0, other * half), (dblk, half))
        return part.reshape(dblk, half // 128, 128).transpose(1, 0, 2).reshape(half, 128)

    pack = jnp.concatenate(
        [
            columns(gate_weight),
            columns(up_weight),
            lax.dynamic_slice(down_weight, (other * half, 0), (half, dblk)),
            mlp_input,
        ],
        axis=0,
    )
    rec = swap(pack)

    dec_rows = up_decoder.shape[0]
    latent_ids = after(latent_ids, chosen)
    slot, rows, rounds = plan(latent_ids, rank, jnp.int32(0), owners, dec_rows)
    picked = jnp.take(up_decoder, rows, axis=0, mode="clip")
    column = exchange(picked, "h")

    cot = jnp.sum(after(cot, column[1]).astype(F32), axis=0).astype(BF16)
    cot = jnp.concatenate([cot[:features], cot[features:]], axis=1)

    used = (half // 128) * (2 * tokens + features)
    padded = -(-used // 128) * 128
    vmem = pl.BlockSpec(memory_space=pltpu.VMEM)
    smem = pl.BlockSpec(memory_space=pltpu.SMEM)
    part = pl.pallas_call(
        functools.partial(forward_kernel, half),
        out_shape=jax.ShapeDtypeStruct((padded, 128), F32),
        in_specs=[smem] + [vmem] * 6,
        out_specs=vmem,
        compiler_params=pltpu.CompilerParams(vmem_limit_bytes=8 * MIB),
    )(core_arg, mlp_input, cot, gate_weight, up_weight, down_weight, rec)
    column = after(jnp.concatenate(column, axis=0), part)
    part = lax.all_to_all(part.reshape(16, padded // 16, 128), ("y", "l"), 0, 0, tiled=True)
    parts = exchange(column, "x")
    part = jnp.sum(part, axis=0)
    slot = after(slot, part)
    pre = lax.all_to_all(
        jnp.broadcast_to(part[None], (16,) + part.shape), ("y", "l"), 0, 0, tiled=True
    ).reshape(padded, 128)

    dec = expand(slot, parts)

    def more(carry):
        return carry[0] < rounds

    def another(carry):
        turn, have = carry
        slot_now, rows_now, _ = plan(latent_ids, rank, turn, owners, dec_rows)
        taken = jnp.take(up_decoder, rows_now, axis=0, mode="clip")
        now = expand(slot_now, exchange(jnp.concatenate(exchange(taken, "h")), "x"))
        here = slot_now.reshape(tokens, slots // 4, 2, 2).transpose(0, 3, 1, 2).reshape(-1, 1)
        return turn + 1, jnp.where(here >= 0, now, have)

    _, dec = lax.while_loop(more, another, (jnp.int32(1), dec))
    dec_far = swap(dec)

    steps = 4
    block = dec.shape[0] // steps
    whole = lambda *shape: pl.BlockSpec(shape, lambda i: (0, 0))
    out_rows = 512
    mine, theirs = pl.pallas_call(
        functools.partial(main_kernel, half, tokens, features),
        grid=(steps,),
        out_shape=(jax.ShapeDtypeStruct((out_rows, 128), F32),) * 2,
        in_specs=[
            smem,
            whole(*pre.shape),
            whole(*gate_weight.shape),
            whole(*up_weight.shape),
            whole(*rec.shape),
            pl.BlockSpec((block, 128), lambda i: (i, 0)),
            pl.BlockSpec((block, 128), lambda i: (i, 0)),
        ],
        out_specs=(whole(out_rows, 128),) * 2,
        scratch_shapes=[
            pltpu.VMEM((2 * dblk, 2 * half), BF16),
            pltpu.VMEM((features * tokens // steps, 2 * half), BF16),
        ],
        compiler_params=pltpu.CompilerParams(vmem_limit_bytes=20 * MIB),
    )(core_arg, pre, gate_weight, up_weight, rec, dec, dec_far)

    total = mine + swap(theirs)
    total = jnp.sum(lax.all_to_all(total.reshape(16, 32, 128), ("x", "y"), 0, 0, tiled=True), axis=0)
    total = jnp.sum(lax.all_to_all(total.reshape(16, 2, 128), ("l", "h"), 0, 0, tiled=True), axis=0)
    total = total.reshape(2, 2, features // 8, tokens // 4).transpose(2, 3, 0, 1)
    return total.reshape(features // 8, tokens // 4, slots // 16) * latent_acts[None, :, :]


def solution(mesh):
    fine = Mesh(mesh.devices.reshape(4, 4, 4, 2, 4), ("x", "h", "y", "c", "l"))
    width = ("y", "c", "l")
    tensor = ("x", "h")
    in_specs = (
        P(None, width),
        P(width, tensor),
        P(width, tensor),
        P(tensor, width),
        P(tensor, width),
        P(),
        P(tensor, width),
        P(),
        P("l", tensor),
    )
    out_specs = P(("y", "c"), "l", tensor)
    return jax.shard_map(
        on_device, mesh=fine, in_specs=in_specs, out_specs=out_specs, check_vma=False
    )
```

```python
import functools

import jax
import jax.numpy as jnp
from jax import lax
from jax.experimental import pallas as pl
from jax.experimental.pallas import tpu as pltpu
from jax.sharding import Mesh
from jax.sharding import PartitionSpec as P

F32 = jnp.float32
BF16 = jnp.bfloat16
CAP = 352
MIB = 1024 * 1024


def nt(a, b):
    return lax.dot_general(a, b, (((1,), (1,)), ((), ())), preferred_element_type=F32)


def nn(a, b):
    return lax.dot_general(a, b, (((1,), (0,)), ((), ())), preferred_element_type=F32)


def plan_kernel(owners, dec_rows, where_ref, ids_ref, slot_ref, list_ref, rounds_ref):
    tokens, slots = ids_ref.shape
    ids = ids_ref[...]
    ids = jnp.concatenate([ids[: tokens // 2], ids[tokens // 2 :]], axis=1)
    rows, lanes = ids.shape
    owner = lax.div(ids, dec_rows)
    upto = lax.broadcasted_iota(jnp.int32, (lanes, lanes), 0) <= lax.broadcasted_iota(
        jnp.int32, (lanes, lanes), 1
    )
    upto = upto.astype(F32).astype(BF16)
    before = lax.broadcasted_iota(jnp.int32, (rows, rows), 1) < lax.broadcasted_iota(
        jnp.int32, (rows, rows), 0
    )
    before = before.astype(F32).astype(BF16)
    ones = jnp.ones((lanes, lanes), BF16)
    pos = jnp.zeros((rows, lanes), F32)
    for o in range(owners):
        hit = (owner == o).astype(F32)
        hit16 = hit.astype(BF16)
        total = nn(hit16, ones).astype(BF16)
        count = nn(hit16, upto) + nn(before, total)
        pos = pos + hit * (count - 1.0)
    rank = where_ref[0]
    start = where_ref[1] * CAP
    at = pos.astype(jnp.int32) - start
    here = jnp.logical_and(at >= 0, at < CAP)
    slot = jnp.where(here, owner * CAP + at, -1)
    slot_ref[...] = jnp.concatenate([slot[:, :slots], slot[:, slots:]], axis=0)
    rounds_ref[0] = lax.div(jnp.max(pos).astype(jnp.int32), CAP) + 1
    mine = jnp.where(owner == rank, pos - start.astype(F32), -1.0)
    local = (ids - rank * dec_rows).astype(F32)
    want = lax.broadcasted_iota(jnp.int32, (CAP, lanes), 0).astype(F32)
    acc = jnp.zeros((CAP, lanes), F32)
    for r in range(rows):
        acc = acc + jnp.where(mine[r : r + 1, :] == want, local[r : r + 1, :], 0.0)
    list_ref[...] = jnp.sum(acc, axis=1, keepdims=True).astype(jnp.int32)


def plan(ids, rank, turn, owners, dec_rows):
    slot, rows, rounds = pl.pallas_call(
        functools.partial(plan_kernel, owners, dec_rows),
        out_shape=(
            jax.ShapeDtypeStruct(ids.shape, jnp.int32),
            jax.ShapeDtypeStruct((CAP, 1), jnp.int32),
            jax.ShapeDtypeStruct((1,), jnp.int32),
        ),
        in_specs=[
            pl.BlockSpec(memory_space=pltpu.SMEM),
            pl.BlockSpec(memory_space=pltpu.VMEM),
        ],
        out_specs=(
            pl.BlockSpec(memory_space=pltpu.VMEM),
            pl.BlockSpec(memory_space=pltpu.VMEM),
            pl.BlockSpec(memory_space=pltpu.SMEM),
        ),
        compiler_params=pltpu.CompilerParams(vmem_limit_bytes=4 * MIB),
    )(jnp.stack([rank, turn]).astype(jnp.int32), ids)
    return slot, rows.reshape(-1), rounds


def expand_kernel(rounds_ref, slot_ref, have_ref, *refs):
    parts, (out_ref, table, block, old, sem) = refs[:-5], refs[-5:]
    size = parts[0].shape[0]
    piece = 128

    def widen(i, carry):
        for p, ref in enumerate(parts):
            to = pl.ds(pl.multiple_of(p * size + i * piece, piece), piece)
            table[to, :] = ref[pl.ds(pl.multiple_of(i * piece, piece), piece), :].astype(F32)
        return carry

    lax.fori_loop(0, size // piece, widen, 0)
    tokens, slots = slot_ref.shape

    def place(low, r, high):
        return low * (slots // 2) + r * 2 + high, r * 4 + high * 2 + low

    order = [place(low, r, high) for low in range(2) for r in range(slots // 4) for high in range(2)]

    def token(t, carry):
        for to, k in order:
            block[to : to + 1, :] = table[pl.ds(slot_ref[t, k], 1), :]
        out_ref[pl.ds(pl.multiple_of(t * slots, slots), slots), :] = block[...].astype(BF16)
        return carry

    def merged(t, carry):
        rows = pl.ds(pl.multiple_of(t * slots, slots), slots)
        copy = pltpu.make_async_copy(have_ref.at[rows], old, sem)
        copy.start()
        copy.wait()
        block[...] = old[...].astype(F32)
        for to, k in order:
            src = slot_ref[t, k]

            @pl.when(src >= 0)
            def _():
                block[to : to + 1, :] = table[pl.ds(src, 1), :]

        out_ref[rows, :] = block[...].astype(BF16)
        return carry

    @pl.when(rounds_ref[0] == 1)
    def _():
        lax.fori_loop(0, tokens, token, 0)

    @pl.when(rounds_ref[0] > 1)
    def _():
        lax.fori_loop(0, tokens, merged, 0)


def expand(rounds, slot, have, parts):
    size = parts[0].shape[0]
    smem = pl.BlockSpec(memory_space=pltpu.SMEM)
    vmem = pl.BlockSpec(memory_space=pltpu.VMEM)
    return pl.pallas_call(
        expand_kernel,
        out_shape=jax.ShapeDtypeStruct(have.shape, BF16),
        in_specs=[smem, smem, pl.BlockSpec(memory_space=pl.ANY)] + [vmem] * len(parts),
        out_specs=vmem,
        scratch_shapes=[
            pltpu.VMEM((len(parts) * size, 128), F32),
            pltpu.VMEM((slot.shape[1], 128), F32),
            pltpu.VMEM((slot.shape[1], 128), BF16),
            pltpu.SemaphoreType.DMA,
        ],
        compiler_params=pltpu.CompilerParams(vmem_limit_bytes=12 * MIB),
    )(rounds, slot, have, *parts)


def tell(value, axis, count):
    return lax.all_to_all(
        jnp.broadcast_to(value[None], (count,) + value.shape), axis, 0, 0, tiled=True
    )


def after(value, other):
    return lax.optimization_barrier((value, other))[0]


def weight_kernel(half, core_ref, gate_ref, up_ref, rec_ref, out_ref):
    dblk = gate_ref.shape[0]
    cols = pl.ds(pl.multiple_of(core_ref[0] * half, 128), half)
    out_ref[:dblk, :half] = gate_ref[:, cols]
    out_ref[:dblk, half:] = up_ref[:, cols]
    for i in range(2 * half // 128):
        out_ref[dblk:, i * 128 : (i + 1) * 128] = rec_ref[i * 128 : (i + 1) * 128, :]


def forward_kernel(half, core_ref, x_ref, cot_ref, weight_ref, down_ref, rec_ref, out_ref):
    core = core_ref[0]
    tokens, dblk = x_ref.shape
    features = cot_ref.shape[0]
    group = 2 * tokens + features
    x = jnp.concatenate([x_ref[...], rec_ref[3 * half : 3 * half + tokens, :]], axis=1)
    pre = nn(x, weight_ref[...])
    down = jnp.concatenate(
        [
            down_ref[pl.ds(pl.multiple_of(core * half, 128), half), :],
            rec_ref[2 * half : 3 * half, :],
        ],
        axis=1,
    )
    neuron = nt(cot_ref[...], down)
    for i in range(half // 128):
        base = i * group
        cols = slice(i * 128, (i + 1) * 128)
        out_ref[base : base + tokens, :] = pre[:, cols]
        out_ref[base + tokens : base + 2 * tokens, :] = pre[:, half + i * 128 : half + (i + 1) * 128]
        out_ref[base + 2 * tokens : base + group, :] = neuron[:, cols]
    used = (half // 128) * group
    if out_ref.shape[0] > used:
        out_ref[used:, :] = jnp.zeros((out_ref.shape[0] - used, 128), F32)


def main_kernel(
    half, tokens, features, steps, core_ref, pre_ref, weight_ref, own_ref, far_ref, mine_ref, theirs_ref,
    dec_ref, grads, sems,
):
    core = core_ref[0]
    tile = tokens // steps
    block = dec_ref.shape[0] // steps
    group = 2 * tokens + features

    def copies(step):
        rows = pl.ds(pl.multiple_of(step * block, block), block)
        return (
            pltpu.make_async_copy(own_ref.at[rows], dec_ref.at[rows, pl.ds(0, 128)], sems.at[step, 0]),
            pltpu.make_async_copy(
                far_ref.at[rows], dec_ref.at[rows, pl.ds(128, 128)], sems.at[step, 1]
            ),
        )

    for step in range(steps):
        for copy in copies(step):
            copy.start()
    lane = lax.broadcasted_iota(jnp.int32, (64, 128), 1)
    first = lax.broadcasted_iota(jnp.int32, (32, 128), 1) < 64
    which = lax.rem(lane, tile)

    def one_step(step, carry):
        for i in range(half // 128):
            base = i * group
            gate_pre = pre_ref[pl.ds(pl.multiple_of(base + step * tile, 8), tile), :]
            up_pre = pre_ref[pl.ds(pl.multiple_of(base + tokens + step * tile, 8), tile), :]
            neuron = pre_ref[base + 2 * tokens : base + group, :]
            s = jax.nn.sigmoid(gate_pre)
            gate_factor = up_pre * s * (1.0 + gate_pre * (1.0 - s))
            up_factor = gate_pre * s
            for j in range(features):
                row = neuron[j : j + 1, :]
                to = slice(j * tile, (j + 1) * tile)
                grads[to, i * 128 : (i + 1) * 128] = (row * gate_factor).astype(BF16)
                grads[to, half + i * 128 : half + (i + 1) * 128] = (row * up_factor).astype(BF16)
        width = nt(grads[...], weight_ref[...])
        high = width.astype(BF16)
        low = (width - high.astype(F32)).astype(BF16)
        for copy in copies(step):
            copy.wait()
        dec = dec_ref[pl.ds(pl.multiple_of(step * block, block), block), :]
        for y in range(features // 8):
            part = slice(y * 128, (y + 1) * 128)
            both = jnp.concatenate([high[part, :], low[part, :]], axis=0)
            full = nt(dec, both)
            full = full[:, :128] + full[:, 128:]
            sel = full[:64, :]
            for t in range(1, tile):
                sel = jnp.where(which == t, full[t * 64 : (t + 1) * 64, :], sel)
            a, b = sel[:32, :], sel[32:, :]
            zero = jnp.where(first, a, pltpu.roll(b, 64, 1))
            one = jnp.where(first, pltpu.roll(a, 64, 1), b)
            keep = jnp.where(core == 0, zero, one)
            send = jnp.where(core == 0, one, zero)
            for x in range(4):
                to = pl.ds(pl.multiple_of(((x * 4 + y) * 4 + step) * 8, 8), 8)
                mine_ref[to, :] = keep[x * 8 : (x + 1) * 8, :]
                theirs_ref[to, :] = send[x * 8 : (x + 1) * 8, :]
        return carry

    lax.fori_loop(0, steps, one_step, 0)


def contract(core_arg, pre, weight, dec, dec_far, half, tokens, features):
    steps = 4
    vmem = pl.BlockSpec(memory_space=pltpu.VMEM)
    hbm = pl.BlockSpec(memory_space=pl.ANY)
    return pl.pallas_call(
        functools.partial(main_kernel, half, tokens, features, steps),
        out_shape=(jax.ShapeDtypeStruct((512, 128), F32),) * 2,
        in_specs=[pl.BlockSpec(memory_space=pltpu.SMEM), vmem, vmem, hbm, hbm],
        out_specs=(vmem,) * 2,
        scratch_shapes=[
            pltpu.VMEM((dec.shape[0], 256), BF16),
            pltpu.VMEM((features * tokens // steps, 2 * half), BF16),
            pltpu.SemaphoreType.DMA((steps, 2)),
        ],
        compiler_params=pltpu.CompilerParams(vmem_limit_bytes=20 * MIB),
    )(core_arg, pre, weight, dec, dec_far)


def swap(value):
    return lax.ppermute(value, "c", [(0, 1), (1, 0)])


def on_device(
    mlp_input,
    gate_weight,
    up_weight,
    down_weight,
    down_encoder,
    feature_ids,
    up_decoder,
    latent_ids,
    latent_acts,
):
    tokens, dblk = mlp_input.shape
    half = gate_weight.shape[1] // 2
    features = feature_ids.shape[0]
    slots = latent_ids.shape[1]
    owners = 16
    core = lax.axis_index("c").astype(jnp.int32)
    rank = (lax.axis_index("x") * 4 + lax.axis_index("h")).astype(jnp.int32)
    core_arg = core[None]
    other = 1 - core

    enc_rows = down_encoder.shape[0]
    local = feature_ids - rank * enc_rows
    picker = (local[:, None] == jnp.arange(enc_rows, dtype=jnp.int32)[None, :]).astype(BF16)
    chosen = jnp.dot(picker, down_encoder, preferred_element_type=F32).astype(BF16)
    other = after(other, chosen)
    chosen = jnp.concatenate([chosen, swap(chosen)], axis=0)

    dec_rows = up_decoder.shape[0]
    slot, rows, rounds = plan(latent_ids, rank, jnp.int32(0), owners, dec_rows)

    def more(carry):
        return carry[0] < rounds[0]

    def another(carry):
        turn, have = carry
        slot_now, rows_now, _ = plan(latent_ids, rank, turn, owners, dec_rows)
        taken = jnp.take(up_decoder, rows_now, axis=0, mode="clip")
        spread = tell(tell(taken, "h", 4).reshape(4 * CAP, 128), "x", 4)
        return turn + 1, expand(rounds, slot_now, have, [spread.reshape(owners * CAP, 128)])

    nothing = jnp.zeros((tokens * slots, 128), BF16)
    _, have = lax.while_loop(more, another, (jnp.int32(1), nothing))
    cot = tell(after(chosen, have), ("x", "h"), owners)

    def columns(w):
        part = lax.dynamic_slice(w, (0, other * half), (dblk, half))
        return part.reshape(dblk, half // 128, 128).transpose(1, 0, 2).reshape(half, 128)

    pack = jnp.concatenate(
        [
            columns(gate_weight),
            columns(up_weight),
            lax.dynamic_slice(down_weight, (other * half, 0), (half, dblk)),
            mlp_input,
        ],
        axis=0,
    )
    rec = swap(pack)

    picked = jnp.take(up_decoder, rows, axis=0, mode="clip")

    table = lax.all_gather(picked, ("x", "h")).reshape(owners * CAP, 128)

    cot = jnp.sum(after(cot, picked).astype(F32), axis=0).astype(BF16)
    cot = jnp.concatenate([cot[:features], cot[features:]], axis=1)

    vmem = pl.BlockSpec(memory_space=pltpu.VMEM)
    smem = pl.BlockSpec(memory_space=pltpu.SMEM)
    weight = pl.pallas_call(
        functools.partial(weight_kernel, half),
        out_shape=jax.ShapeDtypeStruct((2 * dblk, 2 * half), BF16),
        in_specs=[smem] + [vmem] * 3,
        out_specs=vmem,
        compiler_params=pltpu.CompilerParams(vmem_limit_bytes=6 * MIB),
    )(core_arg, gate_weight, up_weight, rec)

    used = (half // 128) * (2 * tokens + features)
    padded = -(-used // 128) * 128
    part = pl.pallas_call(
        functools.partial(forward_kernel, half),
        out_shape=jax.ShapeDtypeStruct((padded, 128), F32),
        in_specs=[smem] + [vmem] * 5,
        out_specs=vmem,
        compiler_params=pltpu.CompilerParams(vmem_limit_bytes=8 * MIB),
    )(core_arg, mlp_input, cot, weight, down_weight, rec)
    part = lax.all_to_all(part.reshape(16, padded // 16, 128), ("y", "l"), 0, 0, tiled=True)
    part = jnp.sum(after(part, table), axis=0)
    slot = after(slot, part)
    pre = lax.all_to_all(
        jnp.broadcast_to(part[None], (16,) + part.shape), ("y", "l"), 0, 0, tiled=True
    ).reshape(padded, 128)

    dec = expand(rounds, slot, have, [table])
    dec_far = swap(dec)

    mine, theirs = contract(core_arg, pre, weight, dec, dec_far, half, tokens, features)

    total = mine + swap(theirs)
    total = jnp.sum(lax.all_to_all(total.reshape(16, 32, 128), ("x", "y"), 0, 0, tiled=True), axis=0)
    total = jnp.sum(lax.all_to_all(total.reshape(16, 2, 128), ("l", "h"), 0, 0, tiled=True), axis=0)
    total = total.reshape(2, 2, features // 8, tokens // 4).transpose(2, 3, 0, 1)
    return total.reshape(features // 8, tokens // 4, slots // 16) * latent_acts[None, :, :]


def solution(mesh):
    fine = Mesh(mesh.devices.reshape(4, 4, 4, 2, 4), ("x", "h", "y", "c", "l"))
    width = ("y", "c", "l")
    tensor = ("x", "h")
    in_specs = (
        P(None, width),
        P(width, tensor),
        P(width, tensor),
        P(tensor, width),
        P(tensor, width),
        P(),
        P(tensor, width),
        P(),
        P("l", tensor),
    )
    out_specs = P(("y", "c"), "l", tensor)
    return jax.shard_map(
        on_device, mesh=fine, in_specs=in_specs, out_specs=out_specs, check_vma=False
    )
```

```python
import functools

import jax
import jax.numpy as jnp
from jax import lax
from jax.experimental import pallas as pl
from jax.experimental.pallas import tpu as pltpu
from jax.sharding import Mesh
from jax.sharding import PartitionSpec as P

F32 = jnp.float32
BF16 = jnp.bfloat16
CAP = 352
MIB = 1024 * 1024


def nt(a, b):
    return lax.dot_general(a, b, (((1,), (1,)), ((), ())), preferred_element_type=F32)


def nn(a, b):
    return lax.dot_general(a, b, (((1,), (0,)), ((), ())), preferred_element_type=F32)


def plan_kernel(owners, dec_rows, where_ref, ids_ref, slot_ref, list_ref, rounds_ref):
    tokens, slots = ids_ref.shape
    ids = ids_ref[...]
    ids = jnp.concatenate([ids[: tokens // 2], ids[tokens // 2 :]], axis=1)
    rows, lanes = ids.shape
    owner = lax.div(ids, dec_rows)
    upto = lax.broadcasted_iota(jnp.int32, (lanes, lanes), 0) <= lax.broadcasted_iota(
        jnp.int32, (lanes, lanes), 1
    )
    upto = upto.astype(F32).astype(BF16)
    before = lax.broadcasted_iota(jnp.int32, (rows, rows), 1) < lax.broadcasted_iota(
        jnp.int32, (rows, rows), 0
    )
    before = before.astype(F32).astype(BF16)
    ones = jnp.ones((lanes, lanes), BF16)
    pos = jnp.zeros((rows, lanes), F32)
    for o in range(owners):
        hit = (owner == o).astype(F32)
        hit16 = hit.astype(BF16)
        total = nn(hit16, ones).astype(BF16)
        count = nn(hit16, upto) + nn(before, total)
        pos = pos + hit * (count - 1.0)
    rank = where_ref[0]
    start = where_ref[1] * CAP
    at = pos.astype(jnp.int32) - start
    here = jnp.logical_and(at >= 0, at < CAP)
    column = lax.bitwise_and(rank, owners - 4)
    slot = jnp.where(here, lax.bitwise_xor(owner, column) * CAP + at, -1)
    slot_ref[...] = jnp.concatenate([slot[:, :slots], slot[:, slots:]], axis=0)
    rounds_ref[0] = lax.div(jnp.max(pos).astype(jnp.int32), CAP) + 1
    mine = jnp.where(owner == rank, pos - start.astype(F32), -1.0)
    local = (ids - rank * dec_rows).astype(F32)
    want = lax.broadcasted_iota(jnp.int32, (CAP, lanes), 0).astype(F32)
    acc = jnp.zeros((CAP, lanes), F32)
    for r in range(rows):
        acc = acc + jnp.where(mine[r : r + 1, :] == want, local[r : r + 1, :], 0.0)
    list_ref[...] = jnp.sum(acc, axis=1, keepdims=True).astype(jnp.int32)


def plan(ids, rank, turn, owners, dec_rows):
    slot, rows, rounds = pl.pallas_call(
        functools.partial(plan_kernel, owners, dec_rows),
        out_shape=(
            jax.ShapeDtypeStruct(ids.shape, jnp.int32),
            jax.ShapeDtypeStruct((CAP, 1), jnp.int32),
            jax.ShapeDtypeStruct((1,), jnp.int32),
        ),
        in_specs=[
            pl.BlockSpec(memory_space=pltpu.SMEM),
            pl.BlockSpec(memory_space=pltpu.VMEM),
        ],
        out_specs=(
            pl.BlockSpec(memory_space=pltpu.VMEM),
            pl.BlockSpec(memory_space=pltpu.VMEM),
            pl.BlockSpec(memory_space=pltpu.SMEM),
        ),
        compiler_params=pltpu.CompilerParams(vmem_limit_bytes=4 * MIB),
    )(jnp.stack([rank, turn]).astype(jnp.int32), ids)
    return slot, rows.reshape(-1), rounds


def expand_kernel(rounds_ref, slot_ref, have_ref, *refs):
    parts, (out_ref, table, block, old, sem) = refs[:-5], refs[-5:]
    size = parts[0].shape[0]
    piece = 128

    def widen(i, carry):
        for p, ref in enumerate(parts):
            to = pl.ds(pl.multiple_of(p * size + i * piece, piece), piece)
            table[to, :] = ref[pl.ds(pl.multiple_of(i * piece, piece), piece), :].astype(F32)
        return carry

    lax.fori_loop(0, size // piece, widen, 0)
    tokens, slots = slot_ref.shape

    def place(low, r, high):
        return low * (slots // 2) + r * 2 + high, r * 4 + high * 2 + low

    order = [place(low, r, high) for low in range(2) for r in range(slots // 4) for high in range(2)]

    def token(t, carry):
        for to, k in order:
            block[to : to + 1, :] = table[pl.ds(slot_ref[t, k], 1), :]
        out_ref[pl.ds(pl.multiple_of(t * slots, slots), slots), :] = block[...].astype(BF16)
        return carry

    def merged(t, carry):
        rows = pl.ds(pl.multiple_of(t * slots, slots), slots)
        copy = pltpu.make_async_copy(have_ref.at[rows], old, sem)
        copy.start()
        copy.wait()
        block[...] = old[...].astype(F32)
        for to, k in order:
            src = slot_ref[t, k]

            @pl.when(src >= 0)
            def _():
                block[to : to + 1, :] = table[pl.ds(src, 1), :]

        out_ref[rows, :] = block[...].astype(BF16)
        return carry

    @pl.when(rounds_ref[0] == 1)
    def _():
        lax.fori_loop(0, tokens, token, 0)

    @pl.when(rounds_ref[0] > 1)
    def _():
        lax.fori_loop(0, tokens, merged, 0)


def expand(rounds, slot, have, parts):
    size = parts[0].shape[0]
    smem = pl.BlockSpec(memory_space=pltpu.SMEM)
    vmem = pl.BlockSpec(memory_space=pltpu.VMEM)
    return pl.pallas_call(
        expand_kernel,
        out_shape=jax.ShapeDtypeStruct(have.shape, BF16),
        in_specs=[smem, smem, pl.BlockSpec(memory_space=pl.ANY)] + [vmem] * len(parts),
        out_specs=vmem,
        scratch_shapes=[
            pltpu.VMEM((len(parts) * size, 128), F32),
            pltpu.VMEM((slot.shape[1], 128), F32),
            pltpu.VMEM((slot.shape[1], 128), BF16),
            pltpu.SemaphoreType.DMA,
        ],
        compiler_params=pltpu.CompilerParams(vmem_limit_bytes=12 * MIB),
    )(rounds, slot, have, *parts)


def exchange(value, axis):
    return [value] + [
        lax.ppermute(value, axis, [(i, i ^ m) for i in range(4)]) for m in range(1, 4)
    ]


def tell(value, axis):
    return lax.all_to_all(jnp.broadcast_to(value[None], (4,) + value.shape), axis, 0, 0, tiled=True)


def after(value, other):
    return lax.optimization_barrier((value, other))[0]


def weight_kernel(half, core_ref, gate_ref, up_ref, rec_ref, out_ref):
    dblk = gate_ref.shape[0]
    cols = pl.ds(pl.multiple_of(core_ref[0] * half, 128), half)
    out_ref[:dblk, :half] = gate_ref[:, cols]
    out_ref[:dblk, half:] = up_ref[:, cols]
    for i in range(2 * half // 128):
        out_ref[dblk:, i * 128 : (i + 1) * 128] = rec_ref[i * 128 : (i + 1) * 128, :]


def forward_kernel(half, core_ref, x_ref, cot_ref, weight_ref, down_ref, rec_ref, out_ref):
    core = core_ref[0]
    tokens, dblk = x_ref.shape
    features = cot_ref.shape[0]
    group = 2 * tokens + features
    x = jnp.concatenate([x_ref[...], rec_ref[3 * half : 3 * half + tokens, :]], axis=1)
    pre = nn(x, weight_ref[...])
    down = jnp.concatenate(
        [
            down_ref[pl.ds(pl.multiple_of(core * half, 128), half), :],
            rec_ref[2 * half : 3 * half, :],
        ],
        axis=1,
    )
    neuron = nt(cot_ref[...], down)
    for i in range(half // 128):
        base = i * group
        cols = slice(i * 128, (i + 1) * 128)
        out_ref[base : base + tokens, :] = pre[:, cols]
        out_ref[base + tokens : base + 2 * tokens, :] = pre[:, half + i * 128 : half + (i + 1) * 128]
        out_ref[base + 2 * tokens : base + group, :] = neuron[:, cols]
    used = (half // 128) * group
    if out_ref.shape[0] > used:
        out_ref[used:, :] = jnp.zeros((out_ref.shape[0] - used, 128), F32)


def main_kernel(
    half, tokens, features, steps, core_ref, pre_ref, weight_ref, own_ref, far_ref, mine_ref, theirs_ref,
    dec_ref, grads, sems,
):
    core = core_ref[0]
    tile = tokens // steps
    block = dec_ref.shape[0] // steps
    group = 2 * tokens + features

    def copies(step):
        rows = pl.ds(pl.multiple_of(step * block, block), block)
        return (
            pltpu.make_async_copy(own_ref.at[rows], dec_ref.at[rows, pl.ds(0, 128)], sems.at[step, 0]),
            pltpu.make_async_copy(
                far_ref.at[rows], dec_ref.at[rows, pl.ds(128, 128)], sems.at[step, 1]
            ),
        )

    for step in range(steps):
        for copy in copies(step):
            copy.start()
    lane = lax.broadcasted_iota(jnp.int32, (64, 128), 1)
    first = lax.broadcasted_iota(jnp.int32, (32, 128), 1) < 64
    which = lax.rem(lane, tile)

    def one_step(step, carry):
        for i in range(half // 128):
            base = i * group
            gate_pre = pre_ref[pl.ds(pl.multiple_of(base + step * tile, 8), tile), :]
            up_pre = pre_ref[pl.ds(pl.multiple_of(base + tokens + step * tile, 8), tile), :]
            neuron = pre_ref[base + 2 * tokens : base + group, :]
            s = jax.nn.sigmoid(gate_pre)
            gate_factor = up_pre * s * (1.0 + gate_pre * (1.0 - s))
            up_factor = gate_pre * s
            for j in range(features):
                row = neuron[j : j + 1, :]
                to = slice(j * tile, (j + 1) * tile)
                grads[to, i * 128 : (i + 1) * 128] = (row * gate_factor).astype(BF16)
                grads[to, half + i * 128 : half + (i + 1) * 128] = (row * up_factor).astype(BF16)
        width = nt(grads[...], weight_ref[...])
        high = width.astype(BF16)
        for copy in copies(step):
            copy.wait()
        dec = dec_ref[pl.ds(pl.multiple_of(step * block, block), block), :]
        for y in range(features // 8):
            if y % 2 == 0:
                pair = nt(dec, high[y * 128 : (y + 2) * 128, :])
            full = pair[:, (y % 2) * 128 : (y % 2 + 1) * 128]
            sel = full[:64, :]
            for t in range(1, tile):
                sel = jnp.where(which == t, full[t * 64 : (t + 1) * 64, :], sel)
            a, b = sel[:32, :], sel[32:, :]
            zero = jnp.where(first, a, pltpu.roll(b, 64, 1))
            one = jnp.where(first, pltpu.roll(a, 64, 1), b)
            keep = jnp.where(core == 0, zero, one)
            send = jnp.where(core == 0, one, zero)
            for x in range(4):
                to = pl.ds(pl.multiple_of(((x * 4 + y) * 4 + step) * 8, 8), 8)
                mine_ref[to, :] = keep[x * 8 : (x + 1) * 8, :]
                theirs_ref[to, :] = send[x * 8 : (x + 1) * 8, :]
        return carry

    lax.fori_loop(0, steps, one_step, 0)


def contract(core_arg, pre, weight, dec, dec_far, half, tokens, features):
    steps = 4
    vmem = pl.BlockSpec(memory_space=pltpu.VMEM)
    hbm = pl.BlockSpec(memory_space=pl.ANY)
    return pl.pallas_call(
        functools.partial(main_kernel, half, tokens, features, steps),
        out_shape=(jax.ShapeDtypeStruct((512, 128), F32),) * 2,
        in_specs=[pl.BlockSpec(memory_space=pltpu.SMEM), vmem, vmem, hbm, hbm],
        out_specs=(vmem,) * 2,
        scratch_shapes=[
            pltpu.VMEM((dec.shape[0], 256), BF16),
            pltpu.VMEM((features * tokens // steps, 2 * half), BF16),
            pltpu.SemaphoreType.DMA((steps, 2)),
        ],
        compiler_params=pltpu.CompilerParams(vmem_limit_bytes=20 * MIB),
    )(core_arg, pre, weight, dec, dec_far)


def swap(value):
    return lax.ppermute(value, "c", [(0, 1), (1, 0)])


def on_device(
    mlp_input,
    gate_weight,
    up_weight,
    down_weight,
    down_encoder,
    feature_ids,
    up_decoder,
    latent_ids,
    latent_acts,
):
    tokens, dblk = mlp_input.shape
    half = gate_weight.shape[1] // 2
    features = feature_ids.shape[0]
    slots = latent_ids.shape[1]
    owners = 16
    core = lax.axis_index("c").astype(jnp.int32)
    rank = (lax.axis_index("x") * 4 + lax.axis_index("h")).astype(jnp.int32)
    core_arg = core[None]
    other = 1 - core

    enc_rows = down_encoder.shape[0]
    local = feature_ids - rank * enc_rows
    picker = (local[:, None] == jnp.arange(enc_rows, dtype=jnp.int32)[None, :]).astype(BF16)
    chosen = jnp.dot(picker, down_encoder, preferred_element_type=F32).astype(BF16)
    other = after(other, chosen)
    chosen = jnp.concatenate([chosen, swap(chosen)], axis=0)

    dec_rows = up_decoder.shape[0]
    slot, rows, rounds = plan(latent_ids, rank, jnp.int32(0), owners, dec_rows)

    def more(carry):
        return carry[0] < rounds[0]

    def another(carry):
        turn, have = carry
        slot_now, rows_now, _ = plan(latent_ids, rank, turn, owners, dec_rows)
        taken = jnp.take(up_decoder, rows_now, axis=0, mode="clip")
        spread = exchange(tell(taken, "h").reshape(4 * CAP, 128), "x")
        return turn + 1, expand(rounds, slot_now, have, spread)

    nothing = jnp.zeros((tokens * slots, 128), BF16)
    _, have = lax.while_loop(more, another, (jnp.int32(1), nothing))
    chosen = tell(after(chosen, have), "x")

    def columns(w):
        part = lax.dynamic_slice(w, (0, other * half), (dblk, half))
        return part.reshape(dblk, half // 128, 128).transpose(1, 0, 2).reshape(half, 128)

    pack = jnp.concatenate(
        [
            columns(gate_weight),
            columns(up_weight),
            lax.dynamic_slice(down_weight, (other * half, 0), (half, dblk)),
            mlp_input,
        ],
        axis=0,
    )
    rec = swap(pack)

    picked = jnp.take(up_decoder, rows, axis=0, mode="clip")

    chosen = jnp.sum(after(chosen, picked).astype(F32), axis=0).astype(BF16)
    packet = tell(jnp.concatenate([picked, chosen], axis=0), "h")
    cot = jnp.sum(packet[:, CAP:, :].astype(F32), axis=0).astype(BF16)
    cot = jnp.concatenate([cot[:features], cot[features:]], axis=1)

    vmem = pl.BlockSpec(memory_space=pltpu.VMEM)
    smem = pl.BlockSpec(memory_space=pltpu.SMEM)
    weight = pl.pallas_call(
        functools.partial(weight_kernel, half),
        out_shape=jax.ShapeDtypeStruct((2 * dblk, 2 * half), BF16),
        in_specs=[smem] + [vmem] * 3,
        out_specs=vmem,
        compiler_params=pltpu.CompilerParams(vmem_limit_bytes=6 * MIB),
    )(core_arg, gate_weight, up_weight, rec)

    used = (half // 128) * (2 * tokens + features)
    padded = -(-used // 128) * 128
    part = pl.pallas_call(
        functools.partial(forward_kernel, half),
        out_shape=jax.ShapeDtypeStruct((padded, 128), F32),
        in_specs=[smem] + [vmem] * 5,
        out_specs=vmem,
        compiler_params=pltpu.CompilerParams(vmem_limit_bytes=8 * MIB),
    )(core_arg, mlp_input, cot, weight, down_weight, rec)
    part, column = lax.optimization_barrier((part, packet[:, :CAP, :].reshape(4 * CAP, 128)))
    part = lax.all_to_all(part.reshape(16, padded // 16, 128), ("y", "l"), 0, 0, tiled=True)
    parts = exchange(column, "x")
    part = jnp.sum(part, axis=0)
    part, slot, parts[1], parts[2] = lax.optimization_barrier((part, slot, parts[1], parts[2]))
    pre = lax.all_to_all(
        jnp.broadcast_to(part[None], (16,) + part.shape), ("y", "l"), 0, 0, tiled=True
    ).reshape(padded, 128)

    dec = expand(rounds, slot, have, parts)
    dec_far = swap(dec)

    mine, theirs = contract(core_arg, pre, weight, dec, dec_far, half, tokens, features)

    total = mine + swap(theirs)
    total = jnp.sum(lax.all_to_all(total.reshape(16, 32, 128), ("x", "y"), 0, 0, tiled=True), axis=0)
    total = jnp.sum(lax.all_to_all(total.reshape(16, 2, 128), ("l", "h"), 0, 0, tiled=True), axis=0)
    total = total.reshape(2, 2, features // 8, tokens // 4).transpose(2, 3, 0, 1)
    return total.reshape(features // 8, tokens // 4, slots // 16) * latent_acts[None, :, :]


def solution(mesh):
    fine = Mesh(mesh.devices.reshape(4, 4, 4, 2, 4), ("x", "h", "y", "c", "l"))
    width = ("y", "c", "l")
    tensor = ("x", "h")
    in_specs = (
        P(None, width),
        P(width, tensor),
        P(width, tensor),
        P(tensor, width),
        P(tensor, width),
        P(),
        P(tensor, width),
        P(),
        P("l", tensor),
    )
    out_specs = P(("y", "c"), "l", tensor)
    return jax.shard_map(
        on_device, mesh=fine, in_specs=in_specs, out_specs=out_specs, check_vma=False
    )
```

```python
import functools

import jax
import jax.numpy as jnp
from jax import lax
from jax.experimental import pallas as pl
from jax.experimental.pallas import tpu as pltpu
from jax.sharding import Mesh
from jax.sharding import PartitionSpec as P

F32 = jnp.float32
BF16 = jnp.bfloat16
CAP = 352
MIB = 1024 * 1024


def nt(a, b):
    return lax.dot_general(a, b, (((1,), (1,)), ((), ())), preferred_element_type=F32)


def nn(a, b):
    return lax.dot_general(a, b, (((1,), (0,)), ((), ())), preferred_element_type=F32)


def plan_kernel(owners, dec_rows, where_ref, ids_ref, slot_ref, here_ref, list_ref, rounds_ref):
    tokens, slots = ids_ref.shape
    ids = ids_ref[...]
    ids = jnp.concatenate([ids[: tokens // 2], ids[tokens // 2 :]], axis=1)
    rows, lanes = ids.shape
    owner = lax.div(ids, dec_rows)
    upto = lax.broadcasted_iota(jnp.int32, (lanes, lanes), 0) <= lax.broadcasted_iota(
        jnp.int32, (lanes, lanes), 1
    )
    upto = upto.astype(F32).astype(BF16)
    before = lax.broadcasted_iota(jnp.int32, (rows, rows), 1) < lax.broadcasted_iota(
        jnp.int32, (rows, rows), 0
    )
    before = before.astype(F32).astype(BF16)
    ones = jnp.ones((lanes, lanes), BF16)
    pos = jnp.zeros((rows, lanes), F32)
    for o in range(owners):
        hit = (owner == o).astype(F32)
        hit16 = hit.astype(BF16)
        total = nn(hit16, ones).astype(BF16)
        count = nn(hit16, upto) + nn(before, total)
        pos = pos + hit * (count - 1.0)
    rank = where_ref[0]
    start = where_ref[1] * CAP
    at = pos.astype(jnp.int32) - start
    here = jnp.logical_and(at >= 0, at < CAP)
    slot = jnp.where(here, lax.bitwise_xor(owner, where_ref[2]) * CAP + at, 0)
    slot_ref[...] = jnp.concatenate([slot[:, :slots], slot[:, slots:]], axis=0)
    here = here.astype(jnp.int32)
    here_ref[...] = jnp.concatenate([here[:, :slots], here[:, slots:]], axis=0)
    rounds_ref[0] = lax.div(jnp.max(pos).astype(jnp.int32), CAP) + 1
    mine = jnp.where(owner == rank, pos - start.astype(F32), -1.0)
    local = (ids - rank * dec_rows).astype(F32)
    want = lax.broadcasted_iota(jnp.int32, (CAP, lanes), 0).astype(F32)
    acc = jnp.zeros((CAP, lanes), F32)
    for r in range(rows):
        acc = acc + jnp.where(mine[r : r + 1, :] == want, local[r : r + 1, :], 0.0)
    list_ref[...] = jnp.sum(acc, axis=1, keepdims=True).astype(jnp.int32)


def plan(ids, rank, turn, flip, owners, dec_rows):
    slot, here, rows, rounds = pl.pallas_call(
        functools.partial(plan_kernel, owners, dec_rows),
        out_shape=(
            jax.ShapeDtypeStruct(ids.shape, jnp.int32),
            jax.ShapeDtypeStruct(ids.shape, jnp.int32),
            jax.ShapeDtypeStruct((CAP, 1), jnp.int32),
            jax.ShapeDtypeStruct((1,), jnp.int32),
        ),
        in_specs=[
            pl.BlockSpec(memory_space=pltpu.SMEM),
            pl.BlockSpec(memory_space=pltpu.VMEM),
        ],
        out_specs=(
            pl.BlockSpec(memory_space=pltpu.VMEM),
            pl.BlockSpec(memory_space=pltpu.VMEM),
            pl.BlockSpec(memory_space=pltpu.VMEM),
            pl.BlockSpec(memory_space=pltpu.SMEM),
        ),
        compiler_params=pltpu.CompilerParams(vmem_limit_bytes=4 * MIB),
    )(jnp.stack([rank, turn, flip]).astype(jnp.int32), ids)
    return slot, here, rows.reshape(-1), rounds[0]


def expand_kernel(slot_ref, *refs):
    parts, (out_ref, table, block) = refs[:-3], refs[-3:]
    size = parts[0].shape[0]
    piece = 128

    def widen(i, carry):
        for p, ref in enumerate(parts):
            to = pl.ds(pl.multiple_of(p * size + i * piece, piece), piece)
            table[to, :] = ref[pl.ds(pl.multiple_of(i * piece, piece), piece), :].astype(F32)
        return carry

    lax.fori_loop(0, size // piece, widen, 0)
    tokens, slots = slot_ref.shape

    def token(t, carry):
        for low in range(2):
            for r in range(slots // 4):
                for high in range(2):
                    src = slot_ref[t, r * 4 + high * 2 + low]
                    to = low * (slots // 2) + r * 2 + high
                    block[to : to + 1, :] = table[pl.ds(src, 1), :]
        out_ref[pl.ds(pl.multiple_of(t * slots, slots), slots), :] = block[...].astype(BF16)
        return carry

    lax.fori_loop(0, tokens, token, 0)


def expand(slot, parts):
    size = parts[0].shape[0]
    vmem = pl.BlockSpec(memory_space=pltpu.VMEM)
    return pl.pallas_call(
        expand_kernel,
        out_shape=jax.ShapeDtypeStruct((slot.shape[0] * slot.shape[1], 128), BF16),
        in_specs=[pl.BlockSpec(memory_space=pltpu.SMEM)] + [vmem] * len(parts),
        out_specs=vmem,
        scratch_shapes=[
            pltpu.VMEM((len(parts) * size, 128), F32),
            pltpu.VMEM((slot.shape[1], 128), F32),
        ],
        compiler_params=pltpu.CompilerParams(vmem_limit_bytes=12 * MIB),
    )(slot, *parts)


def exchange(value, axis):
    return [value] + [
        lax.ppermute(value, axis, [(i, i ^ m) for i in range(4)]) for m in range(1, 4)
    ]


def tell(value, axis):
    return lax.all_to_all(jnp.broadcast_to(value[None], (4,) + value.shape), axis, 0, 0, tiled=True)


def weight_kernel(half, core_ref, gate_ref, up_ref, rec_ref, out_ref):
    dblk = gate_ref.shape[0]
    cols = pl.ds(pl.multiple_of(core_ref[0] * half, 128), half)
    out_ref[:dblk, :half] = gate_ref[:, cols]
    out_ref[:dblk, half:] = up_ref[:, cols]
    for i in range(2 * half // 128):
        out_ref[dblk:, i * 128 : (i + 1) * 128] = rec_ref[i * 128 : (i + 1) * 128, :]


def forward_kernel(half, core_ref, x_ref, cot_ref, weight_ref, down_ref, rec_ref, out_ref):
    core = core_ref[0]
    tokens, dblk = x_ref.shape
    features = cot_ref.shape[0]
    group = 2 * tokens + features
    x = jnp.concatenate([x_ref[...], rec_ref[3 * half : 3 * half + tokens, :]], axis=1)
    pre = nn(x, weight_ref[...])
    down = jnp.concatenate(
        [
            down_ref[pl.ds(pl.multiple_of(core * half, 128), half), :],
            rec_ref[2 * half : 3 * half, :],
        ],
        axis=1,
    )
    neuron = nt(cot_ref[...], down)
    for i in range(half // 128):
        base = i * group
        cols = slice(i * 128, (i + 1) * 128)
        out_ref[base : base + tokens, :] = pre[:, cols]
        out_ref[base + tokens : base + 2 * tokens, :] = pre[:, half + i * 128 : half + (i + 1) * 128]
        out_ref[base + 2 * tokens : base + group, :] = neuron[:, cols]
    used = (half // 128) * group
    if out_ref.shape[0] > used:
        out_ref[used:, :] = jnp.zeros((out_ref.shape[0] - used, 128), F32)


def main_kernel(
    half, tokens, features, steps, core_ref, pre_ref, weight_ref, own_ref, far_ref, mine_ref, theirs_ref,
    dec_ref, grads, sems,
):
    core = core_ref[0]
    tile = tokens // steps
    block = dec_ref.shape[0] // steps
    group = 2 * tokens + features

    def copies(step):
        rows = pl.ds(pl.multiple_of(step * block, block), block)
        return (
            pltpu.make_async_copy(own_ref.at[rows], dec_ref.at[rows, pl.ds(0, 128)], sems.at[step, 0]),
            pltpu.make_async_copy(
                far_ref.at[rows], dec_ref.at[rows, pl.ds(128, 128)], sems.at[step, 1]
            ),
        )

    for step in range(steps):
        for copy in copies(step):
            copy.start()
    lane = lax.broadcasted_iota(jnp.int32, (64, 128), 1)
    first = lax.broadcasted_iota(jnp.int32, (32, 128), 1) < 64
    which = lax.rem(lane, tile)

    def one_step(step, carry):
        for i in range(half // 128):
            base = i * group
            gate_pre = pre_ref[pl.ds(pl.multiple_of(base + step * tile, 8), tile), :]
            up_pre = pre_ref[pl.ds(pl.multiple_of(base + tokens + step * tile, 8), tile), :]
            neuron = pre_ref[base + 2 * tokens : base + group, :]
            s = jax.nn.sigmoid(gate_pre)
            gate_factor = up_pre * s * (1.0 + gate_pre * (1.0 - s))
            up_factor = gate_pre * s
            for j in range(features):
                row = neuron[j : j + 1, :]
                to = slice(j * tile, (j + 1) * tile)
                grads[to, i * 128 : (i + 1) * 128] = (row * gate_factor).astype(BF16)
                grads[to, half + i * 128 : half + (i + 1) * 128] = (row * up_factor).astype(BF16)
        width = nt(grads[...], weight_ref[...])
        high = width.astype(BF16)
        for copy in copies(step):
            copy.wait()
        dec = dec_ref[pl.ds(pl.multiple_of(step * block, block), block), :]
        for y in range(features // 8):
            if y % 2 == 0:
                pair = nt(dec, high[y * 128 : (y + 2) * 128, :])
            full = pair[:, (y % 2) * 128 : (y % 2 + 1) * 128]
            sel = full[:64, :]
            for t in range(1, tile):
                sel = jnp.where(which == t, full[t * 64 : (t + 1) * 64, :], sel)
            a, b = sel[:32, :], sel[32:, :]
            zero = jnp.where(first, a, pltpu.roll(b, 64, 1))
            one = jnp.where(first, pltpu.roll(a, 64, 1), b)
            keep = jnp.where(core == 0, zero, one)
            send = jnp.where(core == 0, one, zero)
            for x in range(4):
                to = pl.ds(pl.multiple_of(((x * 4 + y) * 4 + step) * 8, 8), 8)
                mine_ref[to, :] = keep[x * 8 : (x + 1) * 8, :]
                theirs_ref[to, :] = send[x * 8 : (x + 1) * 8, :]
        return carry

    lax.fori_loop(0, steps, one_step, 0)


def contract(core_arg, pre, weight, dec, dec_far, half, tokens, features):
    steps = 4
    vmem = pl.BlockSpec(memory_space=pltpu.VMEM)
    hbm = pl.BlockSpec(memory_space=pl.ANY)
    return pl.pallas_call(
        functools.partial(main_kernel, half, tokens, features, steps),
        out_shape=(jax.ShapeDtypeStruct((512, 128), F32),) * 2,
        in_specs=[pl.BlockSpec(memory_space=pltpu.SMEM), vmem, vmem, hbm, hbm],
        out_specs=(vmem,) * 2,
        scratch_shapes=[
            pltpu.VMEM((dec.shape[0], 256), BF16),
            pltpu.VMEM((features * tokens // steps, 2 * half), BF16),
            pltpu.SemaphoreType.DMA((steps, 2)),
        ],
        compiler_params=pltpu.CompilerParams(vmem_limit_bytes=20 * MIB),
    )(core_arg, pre, weight, dec, dec_far)


def swap(value):
    return lax.ppermute(value, "c", [(0, 1), (1, 0)])


def on_device(
    mlp_input,
    gate_weight,
    up_weight,
    down_weight,
    down_encoder,
    feature_ids,
    up_decoder,
    latent_ids,
    latent_acts,
):
    tokens, dblk = mlp_input.shape
    half = gate_weight.shape[1] // 2
    features = feature_ids.shape[0]
    slots = latent_ids.shape[1]
    owners = 16
    core = lax.axis_index("c").astype(jnp.int32)
    rank = (lax.axis_index("x") * 4 + lax.axis_index("h")).astype(jnp.int32)
    core_arg = core[None]
    other = 1 - core

    enc_rows = down_encoder.shape[0]
    local = feature_ids - rank * enc_rows
    picker = (local[:, None] == jnp.arange(enc_rows, dtype=jnp.int32)[None, :]).astype(BF16)
    chosen = jnp.dot(picker, down_encoder, preferred_element_type=F32).astype(BF16)
    chosen, other = lax.optimization_barrier((chosen, other))
    chosen = jnp.concatenate([chosen, swap(chosen)], axis=0)
    chosen = tell(chosen, "x")

    def columns(w):
        part = lax.dynamic_slice(w, (0, other * half), (dblk, half))
        return part.reshape(dblk, half // 128, 128).transpose(1, 0, 2).reshape(half, 128)

    pack = jnp.concatenate(
        [
            columns(gate_weight),
            columns(up_weight),
            lax.dynamic_slice(down_weight, (other * half, 0), (half, dblk)),
            mlp_input,
        ],
        axis=0,
    )
    rec = swap(pack)

    dec_rows = up_decoder.shape[0]
    slot, _, rows, rounds = plan(latent_ids, rank, jnp.int32(0), rank // 4 * 4, owners, dec_rows)
    picked = jnp.take(up_decoder, rows, axis=0, mode="clip")
    picked, chosen = lax.optimization_barrier((picked, chosen))
    chosen = jnp.sum(chosen.astype(F32), axis=0).astype(BF16)
    packet = tell(jnp.concatenate([picked, chosen], axis=0), "h")
    column = packet[:, :CAP, :].reshape(4 * CAP, 128)
    cot = jnp.sum(packet[:, CAP:, :].astype(F32), axis=0).astype(BF16)
    cot = jnp.concatenate([cot[:features], cot[features:]], axis=1)

    vmem = pl.BlockSpec(memory_space=pltpu.VMEM)
    smem = pl.BlockSpec(memory_space=pltpu.SMEM)
    weight = pl.pallas_call(
        functools.partial(weight_kernel, half),
        out_shape=jax.ShapeDtypeStruct((2 * dblk, 2 * half), BF16),
        in_specs=[smem] + [vmem] * 3,
        out_specs=vmem,
        compiler_params=pltpu.CompilerParams(vmem_limit_bytes=6 * MIB),
    )(core_arg, gate_weight, up_weight, rec)

    used = (half // 128) * (2 * tokens + features)
    padded = -(-used // 128) * 128
    part = pl.pallas_call(
        functools.partial(forward_kernel, half),
        out_shape=jax.ShapeDtypeStruct((padded, 128), F32),
        in_specs=[smem] + [vmem] * 5,
        out_specs=vmem,
        compiler_params=pltpu.CompilerParams(vmem_limit_bytes=8 * MIB),
    )(core_arg, mlp_input, cot, weight, down_weight, rec)
    part, column = lax.optimization_barrier((part, column))
    part = lax.all_to_all(part.reshape(16, padded // 16, 128), ("y", "l"), 0, 0, tiled=True)
    parts = exchange(column, "x")
    part = jnp.sum(part, axis=0)
    part, slot = lax.optimization_barrier((part, slot))
    pre = lax.all_to_all(
        jnp.broadcast_to(part[None], (16,) + part.shape), ("y", "l"), 0, 0, tiled=True
    ).reshape(padded, 128)

    dec = expand(slot, parts)

    def more(carry):
        return carry[0] < rounds

    def another(carry):
        turn, have = carry
        slot_now, here, rows_now, _ = plan(latent_ids, rank, turn, rank, owners, dec_rows)
        taken = jnp.take(up_decoder, rows_now, axis=0, mode="clip")
        now = expand(slot_now, exchange(jnp.concatenate(exchange(taken, "h"), axis=0), "x"))
        here = here.reshape(tokens, slots // 4, 2, 2).transpose(0, 3, 1, 2).reshape(-1, 1)
        return turn + 1, jnp.where(here > 0, now, have)

    _, dec = lax.while_loop(more, another, (jnp.int32(1), dec))
    dec_far = swap(dec)

    mine, theirs = contract(core_arg, pre, weight, dec, dec_far, half, tokens, features)

    total = mine + swap(theirs)
    total = jnp.sum(lax.all_to_all(total.reshape(16, 32, 128), ("x", "y"), 0, 0, tiled=True), axis=0)
    total = jnp.sum(lax.all_to_all(total.reshape(16, 2, 128), ("l", "h"), 0, 0, tiled=True), axis=0)
    total = total.reshape(2, 2, features // 8, tokens // 4).transpose(2, 3, 0, 1)
    return total.reshape(features // 8, tokens // 4, slots // 16) * latent_acts[None, :, :]


def solution(mesh):
    fine = Mesh(mesh.devices.reshape(4, 4, 4, 2, 4), ("x", "h", "y", "c", "l"))
    width = ("y", "c", "l")
    tensor = ("x", "h")
    in_specs = (
        P(None, width),
        P(width, tensor),
        P(width, tensor),
        P(tensor, width),
        P(tensor, width),
        P(),
        P(tensor, width),
        P(),
        P("l", tensor),
    )
    out_specs = P(("y", "c"), "l", tensor)
    return jax.shard_map(
        on_device, mesh=fine, in_specs=in_specs, out_specs=out_specs, check_vma=False
    )
```

```python
import functools

import jax
import jax.numpy as jnp
from jax import lax
from jax.experimental import pallas as pl
from jax.experimental.pallas import tpu as pltpu
from jax.sharding import Mesh
from jax.sharding import PartitionSpec as P

F32 = jnp.float32
BF16 = jnp.bfloat16
CAP = 352
MIB = 1024 * 1024


def nt(a, b):
    return lax.dot_general(a, b, (((1,), (1,)), ((), ())), preferred_element_type=F32)


def nn(a, b):
    return lax.dot_general(a, b, (((1,), (0,)), ((), ())), preferred_element_type=F32)


def plan_kernel(owners, dec_rows, where_ref, ids_ref, slot_ref, here_ref, list_ref, rounds_ref):
    tokens, slots = ids_ref.shape
    ids = ids_ref[...]
    ids = jnp.concatenate([ids[: tokens // 2], ids[tokens // 2 :]], axis=1)
    rows, lanes = ids.shape
    owner = lax.div(ids, dec_rows)
    upto = lax.broadcasted_iota(jnp.int32, (lanes, lanes), 0) <= lax.broadcasted_iota(
        jnp.int32, (lanes, lanes), 1
    )
    upto = upto.astype(F32).astype(BF16)
    before = lax.broadcasted_iota(jnp.int32, (rows, rows), 1) < lax.broadcasted_iota(
        jnp.int32, (rows, rows), 0
    )
    before = before.astype(F32).astype(BF16)
    ones = jnp.ones((lanes, lanes), BF16)
    pos = jnp.zeros((rows, lanes), F32)
    for o in range(owners):
        hit = (owner == o).astype(F32)
        hit16 = hit.astype(BF16)
        total = nn(hit16, ones).astype(BF16)
        count = nn(hit16, upto) + nn(before, total)
        pos = pos + hit * (count - 1.0)
    rank = where_ref[0]
    start = where_ref[1] * CAP
    at = pos.astype(jnp.int32) - start
    here = jnp.logical_and(at >= 0, at < CAP)
    slot = jnp.where(here, lax.bitwise_xor(owner, where_ref[2]) * CAP + at, 0)
    slot_ref[...] = jnp.concatenate([slot[:, :slots], slot[:, slots:]], axis=0)
    here = here.astype(jnp.int32)
    here_ref[...] = jnp.concatenate([here[:, :slots], here[:, slots:]], axis=0)
    rounds_ref[0] = lax.div(jnp.max(pos).astype(jnp.int32), CAP) + 1
    mine = jnp.where(owner == rank, pos - start.astype(F32), -1.0)
    local = (ids - rank * dec_rows).astype(F32)
    want = lax.broadcasted_iota(jnp.int32, (CAP, lanes), 0).astype(F32)
    acc = jnp.zeros((CAP, lanes), F32)
    for r in range(rows):
        acc = acc + jnp.where(mine[r : r + 1, :] == want, local[r : r + 1, :], 0.0)
    list_ref[...] = jnp.sum(acc, axis=1, keepdims=True).astype(jnp.int32)


def plan(ids, rank, turn, flip, owners, dec_rows):
    slot, here, rows, rounds = pl.pallas_call(
        functools.partial(plan_kernel, owners, dec_rows),
        out_shape=(
            jax.ShapeDtypeStruct(ids.shape, jnp.int32),
            jax.ShapeDtypeStruct(ids.shape, jnp.int32),
            jax.ShapeDtypeStruct((CAP, 1), jnp.int32),
            jax.ShapeDtypeStruct((1,), jnp.int32),
        ),
        in_specs=[
            pl.BlockSpec(memory_space=pltpu.SMEM),
            pl.BlockSpec(memory_space=pltpu.VMEM),
        ],
        out_specs=(
            pl.BlockSpec(memory_space=pltpu.VMEM),
            pl.BlockSpec(memory_space=pltpu.VMEM),
            pl.BlockSpec(memory_space=pltpu.VMEM),
            pl.BlockSpec(memory_space=pltpu.SMEM),
        ),
        compiler_params=pltpu.CompilerParams(vmem_limit_bytes=4 * MIB),
    )(jnp.stack([rank, turn, flip]).astype(jnp.int32), ids)
    return slot, here, rows.reshape(-1), rounds[0]


def expand_kernel(slot_ref, *refs):
    parts, (out_ref, table, block) = refs[:-3], refs[-3:]
    size = parts[0].shape[0]
    piece = 128

    def widen(i, carry):
        for p, ref in enumerate(parts):
            to = pl.ds(pl.multiple_of(p * size + i * piece, piece), piece)
            table[to, :] = ref[pl.ds(pl.multiple_of(i * piece, piece), piece), :].astype(F32)
        return carry

    lax.fori_loop(0, size // piece, widen, 0)
    tokens, slots = slot_ref.shape

    def token(t, carry):
        for low in range(2):
            for r in range(slots // 4):
                for high in range(2):
                    src = slot_ref[t, r * 4 + high * 2 + low]
                    to = low * (slots // 2) + r * 2 + high
                    block[to : to + 1, :] = table[pl.ds(src, 1), :]
        out_ref[pl.ds(pl.multiple_of(t * slots, slots), slots), :] = block[...].astype(BF16)
        return carry

    lax.fori_loop(0, tokens, token, 0)


def expand(slot, parts):
    size = parts[0].shape[0]
    vmem = pl.BlockSpec(memory_space=pltpu.VMEM)
    return pl.pallas_call(
        expand_kernel,
        out_shape=jax.ShapeDtypeStruct((slot.shape[0] * slot.shape[1], 128), BF16),
        in_specs=[pl.BlockSpec(memory_space=pltpu.SMEM)] + [vmem] * len(parts),
        out_specs=vmem,
        scratch_shapes=[
            pltpu.VMEM((len(parts) * size, 128), F32),
            pltpu.VMEM((slot.shape[1], 128), F32),
        ],
        compiler_params=pltpu.CompilerParams(vmem_limit_bytes=12 * MIB),
    )(slot, *parts)


def exchange(value, axis):
    return [value] + [
        lax.ppermute(value, axis, [(i, i ^ m) for i in range(4)]) for m in range(1, 4)
    ]


def tell(value, axis):
    return lax.all_to_all(jnp.broadcast_to(value[None], (4,) + value.shape), axis, 0, 0, tiled=True)


def weight_kernel(half, core_ref, gate_ref, up_ref, rec_ref, out_ref):
    dblk = gate_ref.shape[0]
    cols = pl.ds(pl.multiple_of(core_ref[0] * half, 128), half)
    out_ref[:dblk, :half] = gate_ref[:, cols]
    out_ref[:dblk, half:] = up_ref[:, cols]
    for i in range(2 * half // 128):
        out_ref[dblk:, i * 128 : (i + 1) * 128] = rec_ref[i * 128 : (i + 1) * 128, :]


def forward_kernel(half, core_ref, x_ref, cot_ref, weight_ref, down_ref, rec_ref, out_ref):
    core = core_ref[0]
    tokens, dblk = x_ref.shape
    features = cot_ref.shape[0]
    group = 2 * tokens + features
    x = jnp.concatenate([x_ref[...], rec_ref[3 * half : 3 * half + tokens, :]], axis=1)
    pre = nn(x, weight_ref[...])
    down = jnp.concatenate(
        [
            down_ref[pl.ds(pl.multiple_of(core * half, 128), half), :],
            rec_ref[2 * half : 3 * half, :],
        ],
        axis=1,
    )
    neuron = nt(cot_ref[...], down)
    for i in range(half // 128):
        base = i * group
        cols = slice(i * 128, (i + 1) * 128)
        out_ref[base : base + tokens, :] = pre[:, cols]
        out_ref[base + tokens : base + 2 * tokens, :] = pre[:, half + i * 128 : half + (i + 1) * 128]
        out_ref[base + 2 * tokens : base + group, :] = neuron[:, cols]
    used = (half // 128) * group
    if out_ref.shape[0] > used:
        out_ref[used:, :] = jnp.zeros((out_ref.shape[0] - used, 128), F32)


def main_kernel(
    half, tokens, features, steps, core_ref, pre_ref, weight_ref, own_ref, far_ref, mine_ref, theirs_ref,
    dec_ref, grads, sems,
):
    core = core_ref[0]
    tile = tokens // steps
    block = dec_ref.shape[0] // steps
    group = 2 * tokens + features

    def copies(step):
        rows = pl.ds(pl.multiple_of(step * block, block), block)
        return (
            pltpu.make_async_copy(own_ref.at[rows], dec_ref.at[rows, pl.ds(0, 128)], sems.at[step, 0]),
            pltpu.make_async_copy(
                far_ref.at[rows], dec_ref.at[rows, pl.ds(128, 128)], sems.at[step, 1]
            ),
        )

    for step in range(steps):
        for copy in copies(step):
            copy.start()
    lane = lax.broadcasted_iota(jnp.int32, (64, 128), 1)
    first = lax.broadcasted_iota(jnp.int32, (32, 128), 1) < 64
    which = lax.rem(lane, tile)

    def one_step(step, carry):
        for i in range(half // 128):
            base = i * group
            gate_pre = pre_ref[pl.ds(pl.multiple_of(base + step * tile, 8), tile), :]
            up_pre = pre_ref[pl.ds(pl.multiple_of(base + tokens + step * tile, 8), tile), :]
            neuron = pre_ref[base + 2 * tokens : base + group, :]
            s = jax.nn.sigmoid(gate_pre)
            gate_factor = up_pre * s * (1.0 + gate_pre * (1.0 - s))
            up_factor = gate_pre * s
            for j in range(features):
                row = neuron[j : j + 1, :]
                to = slice(j * tile, (j + 1) * tile)
                grads[to, i * 128 : (i + 1) * 128] = (row * gate_factor).astype(BF16)
                grads[to, half + i * 128 : half + (i + 1) * 128] = (row * up_factor).astype(BF16)
        width = nt(grads[...], weight_ref[...])
        high = width.astype(BF16)
        for copy in copies(step):
            copy.wait()
        dec = dec_ref[pl.ds(pl.multiple_of(step * block, block), block), :]
        for y in range(features // 8):
            if y % 2 == 0:
                pair = nt(dec, high[y * 128 : (y + 2) * 128, :])
            full = pair[:, (y % 2) * 128 : (y % 2 + 1) * 128]
            sel = full[:64, :]
            for t in range(1, tile):
                sel = jnp.where(which == t, full[t * 64 : (t + 1) * 64, :], sel)
            a, b = sel[:32, :], sel[32:, :]
            zero = jnp.where(first, a, pltpu.roll(b, 64, 1))
            one = jnp.where(first, pltpu.roll(a, 64, 1), b)
            keep = jnp.where(core == 0, zero, one)
            send = jnp.where(core == 0, one, zero)
            for x in range(4):
                to = pl.ds(pl.multiple_of(((x * 4 + y) * 4 + step) * 8, 8), 8)
                mine_ref[to, :] = keep[x * 8 : (x + 1) * 8, :]
                theirs_ref[to, :] = send[x * 8 : (x + 1) * 8, :]
        return carry

    lax.fori_loop(0, steps, one_step, 0)


def contract(core_arg, pre, weight, dec, dec_far, half, tokens, features):
    steps = 4
    vmem = pl.BlockSpec(memory_space=pltpu.VMEM)
    hbm = pl.BlockSpec(memory_space=pl.ANY)
    return pl.pallas_call(
        functools.partial(main_kernel, half, tokens, features, steps),
        out_shape=(jax.ShapeDtypeStruct((512, 128), F32),) * 2,
        in_specs=[pl.BlockSpec(memory_space=pltpu.SMEM), vmem, vmem, hbm, hbm],
        out_specs=(vmem,) * 2,
        scratch_shapes=[
            pltpu.VMEM((dec.shape[0], 256), BF16),
            pltpu.VMEM((features * tokens // steps, 2 * half), BF16),
            pltpu.SemaphoreType.DMA((steps, 2)),
        ],
        compiler_params=pltpu.CompilerParams(vmem_limit_bytes=20 * MIB),
    )(core_arg, pre, weight, dec, dec_far)


def swap(value):
    return lax.ppermute(value, "c", [(0, 1), (1, 0)])


def on_device(
    mlp_input,
    gate_weight,
    up_weight,
    down_weight,
    down_encoder,
    feature_ids,
    up_decoder,
    latent_ids,
    latent_acts,
):
    tokens, dblk = mlp_input.shape
    half = gate_weight.shape[1] // 2
    features = feature_ids.shape[0]
    slots = latent_ids.shape[1]
    owners = 16
    core = lax.axis_index("c").astype(jnp.int32)
    rank = (lax.axis_index("x") * 4 + lax.axis_index("h")).astype(jnp.int32)
    core_arg = core[None]
    other = 1 - core

    enc_rows = down_encoder.shape[0]
    local = feature_ids - rank * enc_rows
    picker = (local[:, None] == jnp.arange(enc_rows, dtype=jnp.int32)[None, :]).astype(BF16)
    chosen = jnp.dot(picker, down_encoder, preferred_element_type=F32).astype(BF16)
    chosen, other = lax.optimization_barrier((chosen, other))
    chosen = jnp.concatenate([chosen, swap(chosen)], axis=0)
    told = chosen
    chosen = tell(chosen, "x")

    def columns(w):
        part = lax.dynamic_slice(w, (0, other * half), (dblk, half))
        return part.reshape(dblk, half // 128, 128).transpose(1, 0, 2).reshape(half, 128)

    pack = jnp.concatenate(
        [
            columns(gate_weight),
            columns(up_weight),
            lax.dynamic_slice(down_weight, (other * half, 0), (half, dblk)),
            mlp_input,
        ],
        axis=0,
    )
    rec = swap(pack)

    dec_rows = up_decoder.shape[0]
    latent_ids = lax.optimization_barrier((latent_ids, told))[0]
    slot, _, rows, rounds = plan(latent_ids, rank, jnp.int32(0), rank // 4 * 4, owners, dec_rows)
    picked = jnp.take(up_decoder, rows, axis=0, mode="clip")
    picked, chosen = lax.optimization_barrier((picked, chosen))
    chosen = jnp.sum(chosen.astype(F32), axis=0).astype(BF16)
    packet = tell(jnp.concatenate([picked, chosen], axis=0), "h")
    column = packet[:, :CAP, :].reshape(4 * CAP, 128)
    cot = jnp.sum(packet[:, CAP:, :].astype(F32), axis=0).astype(BF16)
    cot = jnp.concatenate([cot[:features], cot[features:]], axis=1)

    vmem = pl.BlockSpec(memory_space=pltpu.VMEM)
    smem = pl.BlockSpec(memory_space=pltpu.SMEM)
    weight = pl.pallas_call(
        functools.partial(weight_kernel, half),
        out_shape=jax.ShapeDtypeStruct((2 * dblk, 2 * half), BF16),
        in_specs=[smem] + [vmem] * 3,
        out_specs=vmem,
        compiler_params=pltpu.CompilerParams(vmem_limit_bytes=6 * MIB),
    )(core_arg, gate_weight, up_weight, rec)

    used = (half // 128) * (2 * tokens + features)
    padded = -(-used // 128) * 128
    part = pl.pallas_call(
        functools.partial(forward_kernel, half),
        out_shape=jax.ShapeDtypeStruct((padded, 128), F32),
        in_specs=[smem] + [vmem] * 5,
        out_specs=vmem,
        compiler_params=pltpu.CompilerParams(vmem_limit_bytes=8 * MIB),
    )(core_arg, mlp_input, cot, weight, down_weight, rec)
    column = lax.optimization_barrier((column, part))[0]
    part = lax.all_to_all(part.reshape(16, padded // 16, 128), ("y", "l"), 0, 0, tiled=True)
    parts = exchange(column, "x")
    part = jnp.sum(part, axis=0)
    part, slot = lax.optimization_barrier((part, slot))
    pre = lax.all_to_all(
        jnp.broadcast_to(part[None], (16,) + part.shape), ("y", "l"), 0, 0, tiled=True
    ).reshape(padded, 128)

    dec = expand(slot, parts)

    def more(carry):
        return carry[0] < rounds

    def another(carry):
        turn, have = carry
        slot_now, here, rows_now, _ = plan(latent_ids, rank, turn, rank, owners, dec_rows)
        taken = jnp.take(up_decoder, rows_now, axis=0, mode="clip")
        now = expand(slot_now, exchange(jnp.concatenate(exchange(taken, "h"), axis=0), "x"))
        here = here.reshape(tokens, slots // 4, 2, 2).transpose(0, 3, 1, 2).reshape(-1, 1)
        return turn + 1, jnp.where(here > 0, now, have)

    _, dec = lax.while_loop(more, another, (jnp.int32(1), dec))
    dec_far = swap(dec)

    mine, theirs = contract(core_arg, pre, weight, dec, dec_far, half, tokens, features)

    total = mine + swap(theirs)
    total = jnp.sum(lax.all_to_all(total.reshape(16, 32, 128), ("x", "y"), 0, 0, tiled=True), axis=0)
    total = jnp.sum(lax.all_to_all(total.reshape(16, 2, 128), ("l", "h"), 0, 0, tiled=True), axis=0)
    total = total.reshape(2, 2, features // 8, tokens // 4).transpose(2, 3, 0, 1)
    return total.reshape(features // 8, tokens // 4, slots // 16) * latent_acts[None, :, :]


def solution(mesh):
    fine = Mesh(mesh.devices.reshape(4, 4, 4, 2, 4), ("x", "h", "y", "c", "l"))
    width = ("y", "c", "l")
    tensor = ("x", "h")
    in_specs = (
        P(None, width),
        P(width, tensor),
        P(width, tensor),
        P(tensor, width),
        P(tensor, width),
        P(),
        P(tensor, width),
        P(),
        P("l", tensor),
    )
    out_specs = P(("y", "c"), "l", tensor)
    return jax.shard_map(
        on_device, mesh=fine, in_specs=in_specs, out_specs=out_specs, check_vma=False
    )
```
